256 devices in a mesh: row: 16 (over z, x_lo), col: 16 (over x_hi, y, core).
Axes of the slice: x: 4 (x_hi: 2, x_lo: 2; x = x_hi * 2 + x_lo), y: 4, z: 8, core: 2. Of those that a mesh axis runs over, the one named last changes fastest.
Arguments:
- embedding: float32 [32768, 256], P(('row', 'col')), may hold values from -6 to 6
- tiles: bfloat16 [16, 16, 64, 128, 128], P('row', 'col')
- tile_rows: int32 [16, 16, 64], P('row', 'col'), may hold values from 0 to 15
- tile_cols: int32 [16, 16, 64], P('row', 'col'), may hold values from 0 to 15
- counts: int32 [16, 16], P('row', 'col'), may hold values from 1 to 64, as said below
Outputs:
- final: float32 [32768, 256], P(('row', 'col'))
The draws below stay inside these ranges and needn't reach their ends.
Inputs may be any that keep to these rules, and one draw needn't show every extreme that they name: `counts`: some grid block has all 64 slots live.
All inputs are finite; a program needn't handle non-finite values.
Results may differ from the reference program's by a relative error of at most 0.0085.
Values may be sent and summed in bfloat16 or wider, within the bound.
No kernel may reach another device: no remote copies, remote signals or barrier semaphores. Data moves between devices by JAX's collectives and lax.ppermute only.
A program may use at most 64 MiB of HBM per device.

```python
import math
import jax
import jax.numpy as jnp
from jax import lax

D = 256
TILE = 128
ROWS_DEV = 128
TILES_DEV = 64
LAYERS = 3
NODES = 32768
N_ROW = 16
N_COL = 16


def draw_tiles(key, part):
    key = jax.random.fold_in(key, 11)
    value_key, shift_key, extra_key = jax.random.split(key, 3)
    shape = (N_ROW, N_COL, TILES_DEV, TILE, TILE)
    shifts = jax.random.randint(shift_key, (N_ROW, N_COL, TILES_DEV, 1, 1), 0, TILE)
    row_ids = jnp.arange(TILE, dtype=jnp.int32)[:, None]
    col_ids = jnp.arange(TILE, dtype=jnp.int32)[None, :]
    band = (col_ids - row_ids - shifts) % TILE == 0
    extra = jax.random.randint(extra_key, shape, 0, TILE) == 0
    present = jnp.logical_or(band, extra).astype(jnp.float32)
    scale = 1.6 / math.sqrt(2.0 * N_COL * TILES_DEV * TILE / ROWS_DEV)
    values = jax.random.uniform(value_key, shape, jnp.float32, 0.2, 1.8)
    return (scale * values * present).astype(jnp.bfloat16)


def draw_counts(key, part):
    key = jax.random.fold_in(key, 23)
    first, second = jax.random.split(key)
    raw = jax.random.randint(first, (N_ROW * N_COL,), 1, TILES_DEV + 1)
    filled = jnp.maximum(1, raw * raw // TILES_DEV)
    picked = jax.random.randint(second, (), 0, N_ROW * N_COL)
    filled = filled.at[picked].set(TILES_DEV)
    return filled.reshape(N_ROW, N_COL).astype(jnp.int32)


def place_ends(values, stream_key, low, top_value):
    place = [jax.random.randint(jax.random.fold_in(stream_key, axis), (), 0, length) for axis, length in enumerate(values.shape)]
    main_axis = values.shape.index(max(values.shape))
    beside = place[:main_axis] + [(place[main_axis] + 1) % values.shape[main_axis]] + place[main_axis + 1:]
    return values.at[tuple(place)].set(low).at[tuple(beside)].set(top_value)


def levels(own_key, extent, shards, least, high):
    loudness = 1.0
    for position, blocks in shards:
        steps = jax.random.uniform(jax.random.fold_in(jax.random.fold_in(own_key, 6), position), (blocks,), jnp.float32, least / len(shards), high / len(shards))
        loudness = loudness * jnp.repeat(jnp.exp(steps), extent[position] // blocks).reshape((-1,) + (1,) * (len(extent) - 1 - position))
    return loudness


def gaussian(own_key, shape, deviation, reach, cuts=(), kind=jnp.bfloat16):
    result = jax.random.normal(own_key, shape, jnp.float32) * deviation
    if len(cuts) > 0:
        result = levels(own_key, shape, cuts, -0.22, 0.18) * result
    return jnp.clip(result, min=-reach, max=reach).astype(kind)


def setup_inputs(seed: int = 0) -> dict:
    arg_keys = jax.random.split(jax.random.key(seed), 6)
    embedding = gaussian(arg_keys[0], (NODES, D), 1.0, 6.0, ((0, 256),), jnp.float32)
    tiles = draw_tiles(jax.random.fold_in(arg_keys[5], 71), 0)
    tile_rows = place_ends(jax.random.randint(arg_keys[2], (N_ROW, N_COL, TILES_DEV), 0, N_COL * ROWS_DEV // TILE), jax.random.fold_in(arg_keys[2], 1), 0, (N_COL * ROWS_DEV // TILE) - 1).astype(jnp.int32)
    tile_cols = place_ends(jax.random.randint(arg_keys[3], (N_ROW, N_COL, TILES_DEV), 0, N_ROW * ROWS_DEV // TILE), jax.random.fold_in(arg_keys[3], 1), 0, (N_ROW * ROWS_DEV // TILE) - 1).astype(jnp.int32)
    counts = draw_counts(jax.random.fold_in(arg_keys[5], 71), 0)
    return dict(embedding=embedding, tiles=tiles, tile_rows=tile_rows, tile_cols=tile_cols, counts=counts)


def block_partial(panel_tiles, block_tiles, rows, cols, count):
    chosen = panel_tiles[cols]
    prod = jnp.einsum("kab,kbd->kad", block_tiles.astype(jnp.float32), chosen.astype(jnp.float32))
    live = (jnp.arange(block_tiles.shape[0], dtype=jnp.int32) < count).astype(jnp.float32)
    prod = prod * live[:, None, None]
    width = panel_tiles.shape[2]
    summed = jnp.zeros((N_COL * ROWS_DEV // TILE, TILE, width), jnp.float32).at[rows].add(prod)
    return summed.reshape(-1, width).astype(jnp.bfloat16)


def reference(embedding, tiles, tile_rows, tile_cols, counts):
    current = embedding
    total = embedding
    for layer in range(LAYERS):
        grid = current.astype(jnp.bfloat16).reshape(N_ROW, N_COL, ROWS_DEV, D)

        def row_block(i):
            def add_block(acc, j):
                column = lax.dynamic_index_in_dim(grid, j, 1, keepdims=False)
                panel_tiles = column.reshape(-1, TILE, D)
                part = block_partial(panel_tiles, tiles[i, j], tile_rows[i, j], tile_cols[i, j], counts[i, j])
                return acc + part.astype(jnp.float32), None

            acc, unused = lax.scan(add_block, jnp.zeros((N_COL * ROWS_DEV, D), jnp.float32), jnp.arange(N_COL, dtype=jnp.int32))
            return acc

        row_sums = lax.map(row_block, jnp.arange(N_ROW, dtype=jnp.int32))
        current = row_sums.reshape(-1, D)
        total = total + current
    return total / (LAYERS + 1.0)
```

```python
import jax
import jax.numpy as jnp
from jax import lax
from jax.experimental import pallas as pl
from jax.experimental.pallas import tpu as pltpu
from jax.sharding import PartitionSpec as P

LAYERS = 3
MIB = 1024 * 1024


def build_kernel(n_row, n_col, own_at_ref, sib_at_ref, meta_ref, own_ref, sib_ref, dense_ref, acc_ref):
    tile = own_ref.shape[1]
    slots = own_ref.shape[0]
    half = n_col // 2
    ring = n_row // 2
    my_row, my_col = meta_ref[0], meta_ref[1]
    core = my_col & 1
    acc_ref[...] = jnp.zeros_like(acc_ref)

    def add_tiles(at_ref, tiles_ref, sibling):
        def add_tile(k, carry):
            row, col = at_ref[k], at_ref[slots + k]
            row_at = ((row ^ my_col) & 1) * half + (row >> 1)
            ahead = ((col >> 1) + ring - (my_row >> 1)) & (ring - 1)
            away = jnp.where(core == 1, ahead, (ring - ahead) & (ring - 1))
            piece = jnp.maximum(2 * away - 1 + sibling, 0)
            col_at = ((col ^ my_row) & 1) * ring + piece
            if sibling:
                keep = (away > 0) & (away < ring // 2)
            else:
                keep = away <= ring // 2

            @pl.when(keep)
            def _():
                at = (
                    pl.ds(pl.multiple_of(row_at * tile, tile), tile),
                    pl.ds(pl.multiple_of(col_at * tile, tile), tile),
                )
                acc_ref[at] += tiles_ref[k].astype(jnp.float32)

            return carry

        lax.fori_loop(0, at_ref[2 * slots], add_tile, 0)

    add_tiles(own_at_ref, own_ref, 0)
    add_tiles(sib_at_ref, sib_ref, 1)

    def emit(r, carry):
        at = pl.ds(pl.multiple_of(r * tile, tile), tile)
        dense_ref[at, :] = acc_ref[at, :].astype(jnp.bfloat16)
        return carry

    lax.fori_loop(0, dense_ref.shape[0] // tile, emit, 0)


def build_dense(own_at, sib_at, meta, own_tiles, sib_tiles, n_row, n_col):
    tile = own_tiles.shape[1]
    shape = (n_col * tile, n_row * tile)
    smem = pl.BlockSpec(memory_space=pltpu.SMEM)
    vmem = pl.BlockSpec(memory_space=pltpu.VMEM)

    def kernel(*refs):
        build_kernel(n_row, n_col, *refs)

    return pl.pallas_call(
        kernel,
        out_shape=jax.ShapeDtypeStruct(shape, jnp.bfloat16),
        in_specs=[smem, smem, smem, vmem, vmem],
        out_specs=vmem,
        scratch_shapes=[pltpu.VMEM(shape, jnp.float32)],
        compiler_params=pltpu.CompilerParams(vmem_limit_bytes=36 * MIB),
        cost_estimate=pl.CostEstimate(flops=shape[0] * shape[1], bytes_accessed=6 * shape[0] * shape[1], transcendentals=0),
        name="build_dense",
    )(own_at, sib_at, meta, own_tiles, sib_tiles)


def dot_rows(dense_ref, panel_ref, first, n_rows, step, store):
    depth = panel_ref.shape[0]
    lanes = dense_ref.shape[1] - depth if first[1] else 0

    def rows(i, carry):
        at = pl.multiple_of(i * step, step)
        store(at, jnp.dot(
            dense_ref[pl.ds(first[0] + at, step), lanes:lanes + depth],
            panel_ref[...],
            preferred_element_type=jnp.float32,
        ))
        return carry

    lax.fori_loop(0, n_rows // step, rows, 0)


def load_panel(panel_ref, refs):
    at = 0
    for ref in refs:
        rows = ref.shape[0]
        panel_ref[at:at + rows, :] = ref[...]
        at += rows


def head_multiply(dense, pieces):
    n_rows = dense.shape[0]
    depth = sum(piece.shape[0] for piece in pieces)
    width = pieces[0].shape[1]
    vmem = pl.BlockSpec(memory_space=pltpu.VMEM)

    def kernel(dense_ref, *refs):
        out_ref, panel_ref = refs[-2:]
        load_panel(panel_ref, refs[:-2])

        def store(at, value):
            out_ref[pl.ds(at, 512), :] = value

        dot_rows(dense_ref, panel_ref, (0, False), n_rows, 512, store)

    return pl.pallas_call(
        kernel,
        out_shape=jax.ShapeDtypeStruct((n_rows, width), jnp.float32),
        in_specs=[vmem] * (1 + len(pieces)),
        out_specs=vmem,
        scratch_shapes=[pltpu.VMEM((depth, width), jnp.bfloat16)],
        compiler_params=pltpu.CompilerParams(vmem_limit_bytes=24 * MIB),
        cost_estimate=pl.CostEstimate(
            flops=2 * n_rows * depth * width, bytes_accessed=2 * n_rows * depth, transcendentals=0
        ),
        name="head_multiply",
    )(dense, *pieces)


def tail_multiply(dense, head, pieces, half_index, dtype):
    n_rows = dense.shape[0] // 2
    depth = sum(piece.shape[0] for piece in pieces)
    width = pieces[0].shape[1]
    first = half_index * n_rows
    vmem = pl.BlockSpec(memory_space=pltpu.VMEM)

    def kernel(dense_ref, head_ref, *refs):
        out_ref, panel_ref = refs[-2:]
        load_panel(panel_ref, refs[:-2])

        def store(at, value):
            out_ref[pl.ds(at, 512), :] = (value + head_ref[pl.ds(first + at, 512), :]).astype(dtype)

        dot_rows(dense_ref, panel_ref, (first, True), n_rows, 512, store)

    return pl.pallas_call(
        kernel,
        out_shape=jax.ShapeDtypeStruct((n_rows, width), dtype),
        in_specs=[vmem] * (2 + len(pieces)),
        out_specs=vmem,
        scratch_shapes=[pltpu.VMEM((depth, width), jnp.bfloat16)],
        compiler_params=pltpu.CompilerParams(vmem_limit_bytes=24 * MIB),
        cost_estimate=pl.CostEstimate(
            flops=2 * n_rows * depth * width, bytes_accessed=2 * n_rows * depth, transcendentals=0
        ),
        name="tail_multiply",
    )(dense, head, *pieces)


def gather_pieces(own, n_row, n_col, build=None):
    ring = n_row // 2
    rows = own.shape[0]
    flip_x = [(i, i ^ 1) for i in range(n_row)]
    flip_core = [(j, j ^ 1) for j in range(n_col)]

    def onward(piece, by):
        pairs = []
        for i in range(n_row):
            for j in range(n_col):
                step = -by if j & 1 else by
                to = ((i >> 1) + step) % ring * 2 + (i & 1)
                pairs.append((i * n_col + j, to * n_col + j))
        return lax.ppermute(piece, ("row", "col"), pairs)

    sibling = lax.ppermute(own, "col", flip_core)
    both = jnp.concatenate([own, sibling])
    one = onward(both, 1)
    two = onward(both, 2)
    dense = None
    if build is not None:
        two, dense = lax.optimization_barrier((two, build(sibling)))
    near = jnp.concatenate([own, one, two])
    flip_near = lax.ppermute(near, "row", flip_x)
    three = onward(two, 1)
    four = onward(two[:rows], 2)
    far = jnp.concatenate([three, four])
    flip_far = lax.ppermute(far, "row", flip_x)
    return [near, far, flip_near], [flip_far], dense


def per_device(embedding, tiles, tile_rows, tile_cols, counts):
    n_row = lax.axis_size("row")
    n_col = lax.axis_size("col")
    per_dev, width = embedding.shape
    flip_core = [(j, j ^ 1) for j in range(n_col)]
    groups = [list(range(core, n_col, 2)) for core in range(2)]

    meta = jnp.stack([lax.axis_index("row"), lax.axis_index("col")]).astype(jnp.int32)
    own_at = jnp.concatenate([tile_rows[0, 0], tile_cols[0, 0], counts[0]])
    sib_at = lax.ppermute(own_at, "col", flip_core)

    def build(ready):
        own_tiles, ready = lax.optimization_barrier((tiles[0, 0], ready))
        sib_tiles = lax.ppermute(own_tiles, "col", flip_core)
        return build_dense(own_at, sib_at, meta, tiles[0, 0], sib_tiles, n_row, n_col)

    early, late, dense = gather_pieces(embedding.astype(jnp.bfloat16), n_row, n_col, build)
    total = embedding
    for layer in range(LAYERS):
        head = head_multiply(dense, early)
        theirs = tail_multiply(dense, head, late, 1, jnp.bfloat16)
        arrived = lax.ppermute(theirs, "col", flip_core)
        mine = tail_multiply(dense, head, late, 0, jnp.float32)
        pair = (mine + arrived.astype(jnp.float32)).astype(jnp.bfloat16)
        parts = lax.all_to_all(
            pair.reshape(n_col // 2, per_dev, width), "col", split_axis=0, concat_axis=0, axis_index_groups=groups
        )
        current = jnp.sum(parts.astype(jnp.float32), axis=0)
        total = total + current
        if layer + 1 < LAYERS:
            early, late, _ = gather_pieces(current.astype(jnp.bfloat16), n_row, n_col)
    return total / (LAYERS + 1.0)


def solution(mesh):
    return jax.shard_map(
        per_device,
        mesh=mesh,
        in_specs=(
            P(("row", "col"), None),
            P("row", "col", None, None, None),
            P("row", "col", None),
            P("row", "col", None),
            P("row", "col"),
        ),
        out_specs=P(("row", "col"), None),
        check_vma=False,
    )
```

```python
import jax
import jax.numpy as jnp
from jax import lax
from jax.experimental import pallas as pl
from jax.experimental.pallas import tpu as pltpu
from jax.sharding import PartitionSpec as P

LAYERS = 3
MIB = 1024 * 1024


def build_kernel(n_row, n_col, own_at_ref, sib_at_ref, meta_ref, own_ref, sib_ref, dense_ref, acc_ref):
    tile = own_ref.shape[1]
    slots = own_ref.shape[0]
    half = n_col // 2
    ring = n_row // 2
    my_row, my_col = meta_ref[0], meta_ref[1]
    core = my_col & 1
    acc_ref[...] = jnp.zeros_like(acc_ref)

    def add_tiles(at_ref, tiles_ref, sibling):
        def add_tile(k, carry):
            row, col = at_ref[k], at_ref[slots + k]
            row_at = ((row ^ my_col) & 1) * half + (row >> 1)
            ahead = ((col >> 1) + ring - (my_row >> 1)) & (ring - 1)
            away = jnp.where(core == 1, ahead, (ring - ahead) & (ring - 1))
            piece = jnp.maximum(2 * away - 1 + sibling, 0)
            late = 2 * ring - ring // 2
            near_at = jnp.where(piece < ring - 1, piece, late)
            far_at = jnp.where(piece < ring - 3, piece + ring - 1, piece + ring)
            col_at = jnp.where(((col ^ my_row) & 1) == 1, far_at, near_at)
            if sibling:
                keep = (away > 0) & (away < ring // 2)
            else:
                keep = away <= ring // 2

            @pl.when(keep)
            def _():
                at = (
                    pl.ds(pl.multiple_of(row_at * tile, tile), tile),
                    pl.ds(pl.multiple_of(col_at * tile, tile), tile),
                )
                acc_ref[at] += tiles_ref[k].astype(jnp.float32)

            return carry

        lax.fori_loop(0, at_ref[2 * slots], add_tile, 0)

    add_tiles(own_at_ref, own_ref, 0)
    add_tiles(sib_at_ref, sib_ref, 1)

    def emit(r, carry):
        at = pl.ds(pl.multiple_of(r * tile, tile), tile)
        dense_ref[at, :] = acc_ref[at, :].astype(jnp.bfloat16)
        return carry

    lax.fori_loop(0, dense_ref.shape[0] // tile, emit, 0)


def build_dense(own_at, sib_at, meta, own_tiles, sib_tiles, n_row, n_col):
    tile = own_tiles.shape[1]
    shape = (n_col * tile, n_row * tile)
    smem = pl.BlockSpec(memory_space=pltpu.SMEM)
    vmem = pl.BlockSpec(memory_space=pltpu.VMEM)

    def kernel(*refs):
        build_kernel(n_row, n_col, *refs)

    return pl.pallas_call(
        kernel,
        out_shape=jax.ShapeDtypeStruct(shape, jnp.bfloat16),
        in_specs=[smem, smem, smem, vmem, vmem],
        out_specs=vmem,
        scratch_shapes=[pltpu.VMEM(shape, jnp.float32)],
        compiler_params=pltpu.CompilerParams(vmem_limit_bytes=36 * MIB),
        cost_estimate=pl.CostEstimate(flops=shape[0] * shape[1], bytes_accessed=6 * shape[0] * shape[1], transcendentals=0),
        name="build_dense",
    )(own_at, sib_at, meta, own_tiles, sib_tiles)


def dot_rows(dense_ref, panel_ref, first, n_rows, step, store):
    depth = panel_ref.shape[0]
    lanes = dense_ref.shape[1] - depth if first[1] else 0

    def rows(i, carry):
        at = pl.multiple_of(i * step, step)
        store(at, jnp.dot(
            dense_ref[pl.ds(first[0] + at, step), lanes:lanes + depth],
            panel_ref[...],
            preferred_element_type=jnp.float32,
        ))
        return carry

    lax.fori_loop(0, n_rows // step, rows, 0)


def load_panel(panel_ref, refs):
    at = 0
    for ref in refs:
        rows = ref.shape[0]
        panel_ref[at:at + rows, :] = ref[...]
        at += rows


def head_multiply(dense, pieces):
    n_rows = dense.shape[0]
    depth = sum(piece.shape[0] for piece in pieces)
    width = pieces[0].shape[1]
    vmem = pl.BlockSpec(memory_space=pltpu.VMEM)

    def kernel(dense_ref, *refs):
        out_ref, panel_ref = refs[-2:]
        load_panel(panel_ref, refs[:-2])

        def store(at, value):
            out_ref[pl.ds(at, 512), :] = value

        dot_rows(dense_ref, panel_ref, (0, False), n_rows, 512, store)

    return pl.pallas_call(
        kernel,
        out_shape=jax.ShapeDtypeStruct((n_rows, width), jnp.float32),
        in_specs=[vmem] * (1 + len(pieces)),
        out_specs=vmem,
        scratch_shapes=[pltpu.VMEM((depth, width), jnp.bfloat16)],
        compiler_params=pltpu.CompilerParams(vmem_limit_bytes=24 * MIB),
        cost_estimate=pl.CostEstimate(
            flops=2 * n_rows * depth * width, bytes_accessed=2 * n_rows * depth, transcendentals=0
        ),
        name="head_multiply",
    )(dense, *pieces)


def tail_multiply(dense, head, pieces, half_index, dtype):
    n_rows = dense.shape[0] // 2
    depth = sum(piece.shape[0] for piece in pieces)
    width = pieces[0].shape[1]
    first = half_index * n_rows
    vmem = pl.BlockSpec(memory_space=pltpu.VMEM)

    def kernel(dense_ref, head_ref, *refs):
        out_ref, panel_ref = refs[-2:]
        load_panel(panel_ref, refs[:-2])

        def store(at, value):
            out_ref[pl.ds(at, 512), :] = (value + head_ref[pl.ds(first + at, 512), :]).astype(dtype)

        dot_rows(dense_ref, panel_ref, (first, True), n_rows, 512, store)

    return pl.pallas_call(
        kernel,
        out_shape=jax.ShapeDtypeStruct((n_rows, width), dtype),
        in_specs=[vmem] * (2 + len(pieces)),
        out_specs=vmem,
        scratch_shapes=[pltpu.VMEM((depth, width), jnp.bfloat16)],
        compiler_params=pltpu.CompilerParams(vmem_limit_bytes=24 * MIB),
        cost_estimate=pl.CostEstimate(
            flops=2 * n_rows * depth * width, bytes_accessed=2 * n_rows * depth, transcendentals=0
        ),
        name="tail_multiply",
    )(dense, head, *pieces)


def gather_pieces(own, n_row, n_col, build=None):
    ring = n_row // 2
    rows = own.shape[0]
    flip_x = [(i, i ^ 1) for i in range(n_row)]
    flip_core = [(j, j ^ 1) for j in range(n_col)]

    def onward(piece, by, name):
        pairs = []
        for i in range(n_row):
            for j in range(n_col):
                step = -by if j & 1 else by
                to = ((i >> 1) + step) % ring * 2 + (i & 1)
                pairs.append((i * n_col + j, to * n_col + j))
        with jax.named_scope(name):
            return lax.ppermute(piece, ("row", "col"), pairs)

    def over(piece, name):
        with jax.named_scope(name):
            return lax.ppermute(piece, "row", flip_x)

    def swap(piece):
        with jax.named_scope("core_swap"):
            return lax.ppermute(piece, "col", flip_core)

    sibling = swap(own)
    both = jnp.concatenate([own, sibling])
    one = onward(both, 1, "z_one")
    two = onward(both, 2, "z_two")
    three = onward(both, 3, "z_three")
    over_one = over(jnp.concatenate([own, one]), "x_one")
    over_two = over(two, "x_two")
    four = onward(three[:rows], 1, "z_four")
    over_three = over(three, "x_three")
    last, dense = four, None
    if build is not None:
        last, dense = lax.optimization_barrier((four, build(sibling)))
    over_four = over(last, "x_four")
    return [own, one, two, three, over_one, over_two], [four, over_three, over_four], dense


def per_device(embedding, tiles, tile_rows, tile_cols, counts):
    n_row = lax.axis_size("row")
    n_col = lax.axis_size("col")
    per_dev, width = embedding.shape
    flip_core = [(j, j ^ 1) for j in range(n_col)]
    groups = [list(range(core, n_col, 2)) for core in range(2)]

    meta = jnp.stack([lax.axis_index("row"), lax.axis_index("col")]).astype(jnp.int32)
    own_at = jnp.concatenate([tile_rows[0, 0], tile_cols[0, 0], counts[0]])
    with jax.named_scope("place_swap"):
        sib_at = lax.ppermute(own_at, "col", flip_core)

    def build(ready):
        own_tiles, ready = lax.optimization_barrier((tiles[0, 0], ready))
        with jax.named_scope("tile_swap"):
            sib_tiles = lax.ppermute(own_tiles, "col", flip_core)
        return build_dense(own_at, sib_at, meta, tiles[0, 0], sib_tiles, n_row, n_col)

    early, late, dense = gather_pieces(embedding.astype(jnp.bfloat16), n_row, n_col, build)
    total = embedding
    for layer in range(LAYERS):
        head = head_multiply(dense, early)
        theirs = tail_multiply(dense, head, late, 1, jnp.bfloat16)
        with jax.named_scope("partial_swap"):
            arrived = lax.ppermute(theirs, "col", flip_core)
        mine = tail_multiply(dense, head, late, 0, jnp.float32)
        pair = (mine + arrived.astype(jnp.float32)).astype(jnp.bfloat16)
        parts = lax.all_to_all(
            pair.reshape(n_col // 2, per_dev, width), "col", split_axis=0, concat_axis=0, axis_index_groups=groups
        )
        current = jnp.sum(parts.astype(jnp.float32), axis=0)
        total = total + current
        if layer + 1 < LAYERS:
            early, late, _ = gather_pieces(current.astype(jnp.bfloat16), n_row, n_col)
    return total / (LAYERS + 1.0)


def solution(mesh):
    return jax.shard_map(
        per_device,
        mesh=mesh,
        in_specs=(
            P(("row", "col"), None),
            P("row", "col", None, None, None),
            P("row", "col", None),
            P("row", "col", None),
            P("row", "col"),
        ),
        out_specs=P(("row", "col"), None),
        check_vma=False,
    )
```

```python
import jax
import jax.numpy as jnp
from jax import lax
from jax.experimental import pallas as pl
from jax.experimental.pallas import tpu as pltpu
from jax.sharding import PartitionSpec as P

LAYERS = 3
MIB = 1024 * 1024


def build_kernel(n_row, n_col, own_at_ref, sib_at_ref, meta_ref, own_ref, sib_ref, dense_ref, acc_ref):
    tile = own_ref.shape[1]
    slots = own_ref.shape[0]
    half = n_col // 2
    ring = n_row // 2
    my_row, my_col = meta_ref[0], meta_ref[1]
    core = my_col & 1
    acc_ref[...] = jnp.zeros_like(acc_ref)

    def add_tiles(at_ref, tiles_ref, sibling):
        def add_tile(k, carry):
            row, col = at_ref[k], at_ref[slots + k]
            row_at = ((row ^ my_col) & 1) * half + (row >> 1)
            ahead = ((col >> 1) + ring - (my_row >> 1)) & (ring - 1)
            away = jnp.where(core == 1, ahead, (ring - ahead) & (ring - 1))
            piece = jnp.maximum(2 * away - 1 + sibling, 0)
            late = 2 * ring - ring // 2
            near_at = jnp.where(piece < ring - 1, piece, late)
            far_at = jnp.where(piece < ring - 3, piece + ring - 1, piece + ring)
            col_at = jnp.where(((col ^ my_row) & 1) == 1, far_at, near_at)
            if sibling:
                keep = (away > 0) & (away < ring // 2)
            else:
                keep = away <= ring // 2

            @pl.when(keep)
            def _():
                at = (
                    pl.ds(pl.multiple_of(row_at * tile, tile), tile),
                    pl.ds(pl.multiple_of(col_at * tile, tile), tile),
                )
                acc_ref[at] += tiles_ref[k].astype(jnp.float32)

            return carry

        lax.fori_loop(0, at_ref[2 * slots], add_tile, 0)

    add_tiles(own_at_ref, own_ref, 0)
    add_tiles(sib_at_ref, sib_ref, 1)

    def emit(r, carry):
        at = pl.ds(pl.multiple_of(r * tile, tile), tile)
        dense_ref[at, :] = acc_ref[at, :].astype(jnp.bfloat16)
        return carry

    lax.fori_loop(0, dense_ref.shape[0] // tile, emit, 0)


def build_dense(own_at, sib_at, meta, own_tiles, sib_tiles, n_row, n_col):
    tile = own_tiles.shape[1]
    shape = (n_col * tile, n_row * tile)
    smem = pl.BlockSpec(memory_space=pltpu.SMEM)
    vmem = pl.BlockSpec(memory_space=pltpu.VMEM)

    def kernel(*refs):
        build_kernel(n_row, n_col, *refs)

    return pl.pallas_call(
        kernel,
        out_shape=jax.ShapeDtypeStruct(shape, jnp.bfloat16),
        in_specs=[smem, smem, smem, vmem, vmem],
        out_specs=vmem,
        scratch_shapes=[pltpu.VMEM(shape, jnp.float32)],
        compiler_params=pltpu.CompilerParams(vmem_limit_bytes=36 * MIB),
        cost_estimate=pl.CostEstimate(flops=shape[0] * shape[1], bytes_accessed=6 * shape[0] * shape[1], transcendentals=0),
        name="build_dense",
    )(own_at, sib_at, meta, own_tiles, sib_tiles)


def dot_rows(dense_ref, panel_ref, first, n_rows, step, store):
    depth = panel_ref.shape[0]
    lanes = dense_ref.shape[1] - depth if first[1] else 0

    def rows(i, carry):
        at = pl.multiple_of(i * step, step)
        store(at, jnp.dot(
            dense_ref[pl.ds(first[0] + at, step), lanes:lanes + depth],
            panel_ref[...],
            preferred_element_type=jnp.float32,
        ))
        return carry

    lax.fori_loop(0, n_rows // step, rows, 0)


def load_panel(panel_ref, refs):
    at = 0
    for ref in refs:
        rows = ref.shape[0]
        panel_ref[at:at + rows, :] = ref[...]
        at += rows


def head_multiply(dense, pieces):
    n_rows = dense.shape[0]
    depth = sum(piece.shape[0] for piece in pieces)
    width = pieces[0].shape[1]
    vmem = pl.BlockSpec(memory_space=pltpu.VMEM)

    def kernel(dense_ref, *refs):
        out_ref, panel_ref = refs[-2:]
        load_panel(panel_ref, refs[:-2])

        def store(at, value):
            out_ref[pl.ds(at, 512), :] = value

        dot_rows(dense_ref, panel_ref, (0, False), n_rows, 512, store)

    return pl.pallas_call(
        kernel,
        out_shape=jax.ShapeDtypeStruct((n_rows, width), jnp.float32),
        in_specs=[vmem] * (1 + len(pieces)),
        out_specs=vmem,
        scratch_shapes=[pltpu.VMEM((depth, width), jnp.bfloat16)],
        compiler_params=pltpu.CompilerParams(vmem_limit_bytes=24 * MIB),
        cost_estimate=pl.CostEstimate(
            flops=2 * n_rows * depth * width, bytes_accessed=2 * n_rows * depth, transcendentals=0
        ),
        name="head_multiply",
    )(dense, *pieces)


def tail_multiply(dense, head, pieces, half_index, dtype):
    n_rows = dense.shape[0] // 2
    depth = sum(piece.shape[0] for piece in pieces)
    width = pieces[0].shape[1]
    first = half_index * n_rows
    vmem = pl.BlockSpec(memory_space=pltpu.VMEM)

    def kernel(dense_ref, head_ref, *refs):
        out_ref, panel_ref = refs[-2:]
        load_panel(panel_ref, refs[:-2])

        def store(at, value):
            out_ref[pl.ds(at, 512), :] = (value + head_ref[pl.ds(first + at, 512), :]).astype(dtype)

        dot_rows(dense_ref, panel_ref, (first, True), n_rows, 512, store)

    return pl.pallas_call(
        kernel,
        out_shape=jax.ShapeDtypeStruct((n_rows, width), dtype),
        in_specs=[vmem] * (2 + len(pieces)),
        out_specs=vmem,
        scratch_shapes=[pltpu.VMEM((depth, width), jnp.bfloat16)],
        compiler_params=pltpu.CompilerParams(vmem_limit_bytes=24 * MIB),
        cost_estimate=pl.CostEstimate(
            flops=2 * n_rows * depth * width, bytes_accessed=2 * n_rows * depth, transcendentals=0
        ),
        name="tail_multiply",
    )(dense, head, *pieces)


def gather_pieces(own, n_row, n_col, build=None):
    ring = n_row // 2
    rows = own.shape[0]
    flip_x = [(i, i ^ 1) for i in range(n_row)]
    flip_core = [(j, j ^ 1) for j in range(n_col)]

    def onward(piece, by, name):
        pairs = []
        for i in range(n_row):
            for j in range(n_col):
                step = -by if j & 1 else by
                to = ((i >> 1) + step) % ring * 2 + (i & 1)
                pairs.append((i * n_col + j, to * n_col + j))
        with jax.named_scope(name):
            return lax.ppermute(piece, ("row", "col"), pairs)

    def over(piece, name):
        with jax.named_scope(name):
            return lax.ppermute(piece, "row", flip_x)

    def swap(piece):
        with jax.named_scope("core_swap"):
            return lax.ppermute(piece, "col", flip_core)

    sibling = swap(own)
    both = jnp.concatenate([own, sibling])
    over_own = over(own, "x_own")
    one = onward(both, 1, "z_one")
    two = onward(both, 2, "z_two")
    three = onward(both, 3, "z_three")
    one, over_own = lax.optimization_barrier((one, over_own))
    over_one = over(one, "x_one")
    two, one = lax.optimization_barrier((two, one))
    over_two = over(two, "x_two")
    four = onward(two[:rows], 2, "z_four")
    three, two = lax.optimization_barrier((three, two))
    over_three = over(three, "x_three")
    last, dense = four, None
    if build is not None:
        last, dense = lax.optimization_barrier((four, build(sibling)))
    over_four = over(last, "x_four")
    return [own, one, two, three, over_own, over_one, over_two], [four, over_three, over_four], dense


def per_device(embedding, tiles, tile_rows, tile_cols, counts):
    n_row = lax.axis_size("row")
    n_col = lax.axis_size("col")
    per_dev, width = embedding.shape
    flip_core = [(j, j ^ 1) for j in range(n_col)]
    groups = [list(range(core, n_col, 2)) for core in range(2)]

    meta = jnp.stack([lax.axis_index("row"), lax.axis_index("col")]).astype(jnp.int32)
    own_at = jnp.concatenate([tile_rows[0, 0], tile_cols[0, 0], counts[0]])
    with jax.named_scope("place_swap"):
        sib_at = lax.ppermute(own_at, "col", flip_core)

    def build(ready):
        own_tiles, ready = lax.optimization_barrier((tiles[0, 0], ready))
        with jax.named_scope("tile_swap"):
            sib_tiles = lax.ppermute(own_tiles, "col", flip_core)
        return build_dense(own_at, sib_at, meta, tiles[0, 0], sib_tiles, n_row, n_col)

    early, late, dense = gather_pieces(embedding.astype(jnp.bfloat16), n_row, n_col, build)
    total = embedding
    for layer in range(LAYERS):
        head = head_multiply(dense, early)
        theirs = tail_multiply(dense, head, late, 1, jnp.bfloat16)
        with jax.named_scope("partial_swap"):
            arrived = lax.ppermute(theirs, "col", flip_core)
        mine = tail_multiply(dense, head, late, 0, jnp.float32)
        pair = (mine + arrived.astype(jnp.float32)).astype(jnp.bfloat16)
        parts = lax.all_to_all(
            pair.reshape(n_col // 2, per_dev, width), "col", split_axis=0, concat_axis=0, axis_index_groups=groups
        )
        current = jnp.sum(parts.astype(jnp.float32), axis=0)
        total = total + current
        if layer + 1 < LAYERS:
            early, late, _ = gather_pieces(current.astype(jnp.bfloat16), n_row, n_col)
    return total / (LAYERS + 1.0)


def solution(mesh):
    return jax.shard_map(
        per_device,
        mesh=mesh,
        in_specs=(
            P(("row", "col"), None),
            P("row", "col", None, None, None),
            P("row", "col", None),
            P("row", "col", None),
            P("row", "col"),
        ),
        out_specs=P(("row", "col"), None),
        check_vma=False,
    )
```

```python
import jax
import jax.numpy as jnp
from jax import lax
from jax.experimental import pallas as pl
from jax.experimental.pallas import tpu as pltpu
from jax.sharding import PartitionSpec as P

LAYERS = 3
MIB = 1024 * 1024


def build_kernel(n_row, n_col, own_at_ref, sib_at_ref, meta_ref, own_ref, sib_ref, dense_ref, acc_ref):
    tile = own_ref.shape[1]
    slots = own_ref.shape[0]
    half = n_col // 2
    ring = n_row // 2
    my_row, my_col = meta_ref[0], meta_ref[1]
    core = my_col & 1
    acc_ref[...] = jnp.zeros_like(acc_ref)

    def add_tiles(at_ref, tiles_ref, sibling):
        def add_tile(k, carry):
            row, col = at_ref[k], at_ref[slots + k]
            row_at = ((row ^ my_col) & 1) * half + (row >> 1)
            ahead = ((col >> 1) + ring - (my_row >> 1)) & (ring - 1)
            away = jnp.where(core == 1, ahead, (ring - ahead) & (ring - 1))
            piece = jnp.maximum(2 * away - 1 + sibling, 0)
            late = 2 * ring - ring // 2
            near_at = jnp.where(piece < ring - 1, piece, late)
            far_at = jnp.where(piece < ring - 3, piece + ring - 1, piece + ring)
            col_at = jnp.where(((col ^ my_row) & 1) == 1, far_at, near_at)
            if sibling:
                keep = (away > 0) & (away < ring // 2)
            else:
                keep = away <= ring // 2

            @pl.when(keep)
            def _():
                at = (
                    pl.ds(pl.multiple_of(row_at * tile, tile), tile),
                    pl.ds(pl.multiple_of(col_at * tile, tile), tile),
                )
                acc_ref[at] += tiles_ref[k].astype(jnp.float32)

            return carry

        lax.fori_loop(0, at_ref[2 * slots], add_tile, 0)

    add_tiles(own_at_ref, own_ref, 0)
    add_tiles(sib_at_ref, sib_ref, 1)

    def emit(r, carry):
        at = pl.ds(pl.multiple_of(r * tile, tile), tile)
        dense_ref[at, :] = acc_ref[at, :].astype(jnp.bfloat16)
        return carry

    lax.fori_loop(0, dense_ref.shape[0] // tile, emit, 0)


def build_dense(own_at, sib_at, meta, own_tiles, sib_tiles, n_row, n_col):
    tile = own_tiles.shape[1]
    shape = (n_col * tile, n_row * tile)
    smem = pl.BlockSpec(memory_space=pltpu.SMEM)
    vmem = pl.BlockSpec(memory_space=pltpu.VMEM)

    def kernel(*refs):
        build_kernel(n_row, n_col, *refs)

    return pl.pallas_call(
        kernel,
        out_shape=jax.ShapeDtypeStruct(shape, jnp.bfloat16),
        in_specs=[smem, smem, smem, vmem, vmem],
        out_specs=vmem,
        scratch_shapes=[pltpu.VMEM(shape, jnp.float32)],
        compiler_params=pltpu.CompilerParams(vmem_limit_bytes=36 * MIB),
        cost_estimate=pl.CostEstimate(flops=shape[0] * shape[1], bytes_accessed=6 * shape[0] * shape[1], transcendentals=0),
        name="build_dense",
    )(own_at, sib_at, meta, own_tiles, sib_tiles)


def dot_rows(dense_ref, panel_ref, first, n_rows, step, store):
    depth = panel_ref.shape[0]
    lanes = dense_ref.shape[1] - depth if first[1] else 0

    def rows(i, carry):
        at = pl.multiple_of(i * step, step)
        store(at, jnp.dot(
            dense_ref[pl.ds(first[0] + at, step), lanes:lanes + depth],
            panel_ref[...],
            preferred_element_type=jnp.float32,
        ))
        return carry

    lax.fori_loop(0, n_rows // step, rows, 0)


def load_panel(panel_ref, refs):
    at = 0
    for ref in refs:
        rows = ref.shape[0]
        panel_ref[at:at + rows, :] = ref[...]
        at += rows


def head_multiply(dense, pieces):
    n_rows = dense.shape[0]
    depth = sum(piece.shape[0] for piece in pieces)
    width = pieces[0].shape[1]
    vmem = pl.BlockSpec(memory_space=pltpu.VMEM)

    def kernel(dense_ref, *refs):
        out_ref, panel_ref = refs[-2:]
        load_panel(panel_ref, refs[:-2])

        def store(at, value):
            out_ref[pl.ds(at, 512), :] = value

        dot_rows(dense_ref, panel_ref, (0, False), n_rows, 512, store)

    return pl.pallas_call(
        kernel,
        out_shape=jax.ShapeDtypeStruct((n_rows, width), jnp.float32),
        in_specs=[vmem] * (1 + len(pieces)),
        out_specs=vmem,
        scratch_shapes=[pltpu.VMEM((depth, width), jnp.bfloat16)],
        compiler_params=pltpu.CompilerParams(vmem_limit_bytes=24 * MIB),
        cost_estimate=pl.CostEstimate(
            flops=2 * n_rows * depth * width, bytes_accessed=2 * n_rows * depth, transcendentals=0
        ),
        name="head_multiply",
    )(dense, *pieces)


def tail_multiply(dense, head, pieces, half_index, dtype):
    n_rows = dense.shape[0] // 2
    depth = sum(piece.shape[0] for piece in pieces)
    width = pieces[0].shape[1]
    first = half_index * n_rows
    vmem = pl.BlockSpec(memory_space=pltpu.VMEM)

    def kernel(dense_ref, head_ref, *refs):
        out_ref, panel_ref = refs[-2:]
        load_panel(panel_ref, refs[:-2])

        def store(at, value):
            out_ref[pl.ds(at, 512), :] = (value + head_ref[pl.ds(first + at, 512), :]).astype(dtype)

        dot_rows(dense_ref, panel_ref, (first, True), n_rows, 512, store)

    return pl.pallas_call(
        kernel,
        out_shape=jax.ShapeDtypeStruct((n_rows, width), dtype),
        in_specs=[vmem] * (2 + len(pieces)),
        out_specs=vmem,
        scratch_shapes=[pltpu.VMEM((depth, width), jnp.bfloat16)],
        compiler_params=pltpu.CompilerParams(vmem_limit_bytes=24 * MIB),
        cost_estimate=pl.CostEstimate(
            flops=2 * n_rows * depth * width, bytes_accessed=2 * n_rows * depth, transcendentals=0
        ),
        name="tail_multiply",
    )(dense, head, *pieces)


def gather_pieces(own, n_row, n_col, build=None):
    ring = n_row // 2
    rows = own.shape[0]
    flip_x = [(i, i ^ 1) for i in range(n_row)]
    flip_core = [(j, j ^ 1) for j in range(n_col)]

    def onward(piece, by, name):
        pairs = []
        for i in range(n_row):
            for j in range(n_col):
                step = -by if j & 1 else by
                to = ((i >> 1) + step) % ring * 2 + (i & 1)
                pairs.append((i * n_col + j, to * n_col + j))
        with jax.named_scope(name):
            return lax.ppermute(piece, ("row", "col"), pairs)

    def over(piece, name):
        with jax.named_scope(name):
            return lax.ppermute(piece, "row", flip_x)

    def swap(piece):
        with jax.named_scope("core_swap"):
            return lax.ppermute(piece, "col", flip_core)

    sibling = swap(own)
    both = jnp.concatenate([own, sibling])
    over_own = over(own, "x_own")
    one = onward(both, 1, "z_one")
    two = onward(both, 2, "z_two")
    three = onward(both, 3, "z_three")
    if build is None:
        four = onward(own, 4, "z_four")
        one, over_own = lax.optimization_barrier((one, over_own))
        over_one = over(one, "x_one")
        two, one = lax.optimization_barrier((two, one))
        over_two = over(two, "x_two")
        three, two = lax.optimization_barrier((three, two))
        far = jnp.concatenate([three, four])
        over_far = over(far, "x_far")
        return [own, one, two, three, over_own, over_one, over_two], [four, over_far], None
    one, over_own = lax.optimization_barrier((one, over_own))
    over_one = over(one, "x_one")
    two, one = lax.optimization_barrier((two, one))
    over_two = over(two, "x_two")
    four = onward(two[:rows], 2, "z_four")
    three, two = lax.optimization_barrier((three, two))
    over_three = over(three, "x_three")
    last, dense = lax.optimization_barrier((four, build(sibling)))
    over_four = over(last, "x_four")
    return [own, one, two, three, over_own, over_one, over_two], [four, over_three, over_four], dense


def per_device(embedding, tiles, tile_rows, tile_cols, counts):
    n_row = lax.axis_size("row")
    n_col = lax.axis_size("col")
    per_dev, width = embedding.shape
    flip_core = [(j, j ^ 1) for j in range(n_col)]
    groups = [list(range(core, n_col, 2)) for core in range(2)]

    meta = jnp.stack([lax.axis_index("row"), lax.axis_index("col")]).astype(jnp.int32)
    own_at = jnp.concatenate([tile_rows[0, 0], tile_cols[0, 0], counts[0]])
    with jax.named_scope("place_swap"):
        sib_at = lax.ppermute(own_at, "col", flip_core)

    def build(ready):
        own_tiles, ready = lax.optimization_barrier((tiles[0, 0], ready))
        with jax.named_scope("tile_swap"):
            sib_tiles = lax.ppermute(own_tiles, "col", flip_core)
        with jax.named_scope("tile_stay"):
            own_tiles = lax.ppermute(own_tiles, "col", [(j, j) for j in range(n_col)])
        return build_dense(own_at, sib_at, meta, own_tiles, sib_tiles, n_row, n_col)

    early, late, dense = gather_pieces(embedding.astype(jnp.bfloat16), n_row, n_col, build)
    total = embedding
    for layer in range(LAYERS):
        head = head_multiply(dense, early)
        theirs = tail_multiply(dense, head, late, 1, jnp.bfloat16)
        with jax.named_scope("partial_swap"):
            arrived = lax.ppermute(theirs, "col", flip_core)
        mine = tail_multiply(dense, head, late, 0, jnp.float32)
        pair = (mine + arrived.astype(jnp.float32)).astype(jnp.bfloat16)
        parts = lax.all_to_all(
            pair.reshape(n_col // 2, per_dev, width), "col", split_axis=0, concat_axis=0, axis_index_groups=groups
        )
        current = jnp.sum(parts.astype(jnp.float32), axis=0)
        total = total + current
        if layer + 1 < LAYERS:
            early, late, _ = gather_pieces(current.astype(jnp.bfloat16), n_row, n_col)
    return total / (LAYERS + 1.0)


def solution(mesh):
    return jax.shard_map(
        per_device,
        mesh=mesh,
        in_specs=(
            P(("row", "col"), None),
            P("row", "col", None, None, None),
            P("row", "col", None),
            P("row", "col", None),
            P("row", "col"),
        ),
        out_specs=P(("row", "col"), None),
        check_vma=False,
    )
```

```python
import jax
import jax.numpy as jnp
from jax import lax
from jax.experimental import pallas as pl
from jax.experimental.pallas import tpu as pltpu
from jax.sharding import PartitionSpec as P

LAYERS = 3
MIB = 1024 * 1024


def build_kernel(n_row, n_col, own_at_ref, sib_at_ref, meta_ref, own_ref, sib_ref, dense_ref, acc_ref):
    tile = own_ref.shape[1]
    slots = own_ref.shape[0]
    half = n_col // 2
    ring = n_row // 2
    my_row, my_col = meta_ref[0], meta_ref[1]
    core = my_col & 1
    acc_ref[...] = jnp.zeros_like(acc_ref)

    def add_tiles(at_ref, tiles_ref, sibling):
        def add_tile(k, carry):
            row, col = at_ref[k], at_ref[slots + k]
            row_at = ((row ^ my_col) & 1) * half + (row >> 1)
            ahead = ((col >> 1) + ring - (my_row >> 1)) & (ring - 1)
            away = jnp.where(core == 1, ahead, (ring - ahead) & (ring - 1))
            piece = jnp.maximum(2 * away - 1 + sibling, 0)
            col_at = ((col ^ my_row) & 1) * ring + piece
            if sibling:
                keep = (away > 0) & (away < ring // 2)
            else:
                keep = away <= ring // 2

            @pl.when(keep)
            def _():
                at = (
                    pl.ds(pl.multiple_of(row_at * tile, tile), tile),
                    pl.ds(pl.multiple_of(col_at * tile, tile), tile),
                )
                acc_ref[at] += tiles_ref[k].astype(jnp.float32)

            return carry

        lax.fori_loop(0, at_ref[2 * slots], add_tile, 0)

    add_tiles(own_at_ref, own_ref, 0)
    add_tiles(sib_at_ref, sib_ref, 1)

    def emit(r, carry):
        at = pl.ds(pl.multiple_of(r * tile, tile), tile)
        dense_ref[at, :] = acc_ref[at, :].astype(jnp.bfloat16)
        return carry

    lax.fori_loop(0, dense_ref.shape[0] // tile, emit, 0)


def build_dense(own_at, sib_at, meta, own_tiles, sib_tiles, n_row, n_col):
    tile = own_tiles.shape[1]
    shape = (n_col * tile, n_row * tile)
    smem = pl.BlockSpec(memory_space=pltpu.SMEM)
    vmem = pl.BlockSpec(memory_space=pltpu.VMEM)

    def kernel(*refs):
        build_kernel(n_row, n_col, *refs)

    return pl.pallas_call(
        kernel,
        out_shape=jax.ShapeDtypeStruct(shape, jnp.bfloat16),
        in_specs=[smem, smem, smem, vmem, vmem],
        out_specs=vmem,
        scratch_shapes=[pltpu.VMEM(shape, jnp.float32)],
        compiler_params=pltpu.CompilerParams(vmem_limit_bytes=36 * MIB),
        cost_estimate=pl.CostEstimate(flops=shape[0] * shape[1], bytes_accessed=6 * shape[0] * shape[1], transcendentals=0),
        name="build_dense",
    )(own_at, sib_at, meta, own_tiles, sib_tiles)


def dot_rows(dense_ref, panel_ref, first, n_rows, step, store):
    depth = panel_ref.shape[0]
    lanes = dense_ref.shape[1] - depth if first[1] else 0

    def rows(i, carry):
        at = pl.multiple_of(i * step, step)
        store(at, jnp.dot(
            dense_ref[pl.ds(first[0] + at, step), lanes:lanes + depth],
            panel_ref[...],
            preferred_element_type=jnp.float32,
        ))
        return carry

    lax.fori_loop(0, n_rows // step, rows, 0)


def load_panel(panel_ref, refs):
    at = 0
    for ref in refs:
        rows = ref.shape[0]
        panel_ref[at:at + rows, :] = ref[...]
        at += rows


def head_multiply(dense, pieces):
    n_rows = dense.shape[0]
    depth = sum(piece.shape[0] for piece in pieces)
    width = pieces[0].shape[1]
    vmem = pl.BlockSpec(memory_space=pltpu.VMEM)

    def kernel(dense_ref, *refs):
        out_ref, panel_ref = refs[-2:]
        load_panel(panel_ref, refs[:-2])

        def store(at, value):
            out_ref[pl.ds(at, 512), :] = value

        dot_rows(dense_ref, panel_ref, (0, False), n_rows, 512, store)

    return pl.pallas_call(
        kernel,
        out_shape=jax.ShapeDtypeStruct((n_rows, width), jnp.float32),
        in_specs=[vmem] * (1 + len(pieces)),
        out_specs=vmem,
        scratch_shapes=[pltpu.VMEM((depth, width), jnp.bfloat16)],
        compiler_params=pltpu.CompilerParams(vmem_limit_bytes=24 * MIB),
        cost_estimate=pl.CostEstimate(
            flops=2 * n_rows * depth * width, bytes_accessed=2 * n_rows * depth, transcendentals=0
        ),
        name="head_multiply",
    )(dense, *pieces)


def tail_multiply(dense, head, pieces, half_index, dtype):
    n_rows = dense.shape[0] // 2
    depth = sum(piece.shape[0] for piece in pieces)
    width = pieces[0].shape[1]
    first = half_index * n_rows
    vmem = pl.BlockSpec(memory_space=pltpu.VMEM)

    def kernel(dense_ref, head_ref, *refs):
        out_ref, panel_ref = refs[-2:]
        load_panel(panel_ref, refs[:-2])

        def store(at, value):
            out_ref[pl.ds(at, 512), :] = (value + head_ref[pl.ds(first + at, 512), :]).astype(dtype)

        dot_rows(dense_ref, panel_ref, (first, True), n_rows, 512, store)

    return pl.pallas_call(
        kernel,
        out_shape=jax.ShapeDtypeStruct((n_rows, width), dtype),
        in_specs=[vmem] * (2 + len(pieces)),
        out_specs=vmem,
        scratch_shapes=[pltpu.VMEM((depth, width), jnp.bfloat16)],
        compiler_params=pltpu.CompilerParams(vmem_limit_bytes=24 * MIB),
        cost_estimate=pl.CostEstimate(
            flops=2 * n_rows * depth * width, bytes_accessed=2 * n_rows * depth, transcendentals=0
        ),
        name="tail_multiply",
    )(dense, head, *pieces)


def gather_pieces(own, n_row, n_col, build=None):
    ring = n_row // 2
    rows = own.shape[0]
    flip_x = [(i, i ^ 1) for i in range(n_row)]
    flip_core = [(j, j ^ 1) for j in range(n_col)]

    def onward(piece, by):
        pairs = []
        for i in range(n_row):
            for j in range(n_col):
                step = -by if j & 1 else by
                to = ((i >> 1) + step) % ring * 2 + (i & 1)
                pairs.append((i * n_col + j, to * n_col + j))
        return lax.ppermute(piece, ("row", "col"), pairs)

    def over(piece):
        return lax.ppermute(piece, "row", flip_x)

    sibling = lax.ppermute(own, "col", flip_core)
    both = jnp.concatenate([own, sibling])
    one = onward(both, 1)
    two = onward(both, 2)
    dense = None
    if build is not None:
        two, dense = lax.optimization_barrier((two, build(sibling)))
        over_near = [over(jnp.concatenate([own, one, two]))]
    else:
        two, over_own = lax.optimization_barrier((two, over(own)))
        over_near = [over_own, over(jnp.concatenate([one, two]))]
    three = onward(two, 1)
    four = onward(two[:rows], 2)
    far = jnp.concatenate([three, four])
    return [own, one, two, far] + over_near, [over(far)], dense


def per_device(embedding, tiles, tile_rows, tile_cols, counts):
    n_row = lax.axis_size("row")
    n_col = lax.axis_size("col")
    per_dev, width = embedding.shape
    flip_core = [(j, j ^ 1) for j in range(n_col)]
    groups = [list(range(core, n_col, 2)) for core in range(2)]

    meta = jnp.stack([lax.axis_index("row"), lax.axis_index("col")]).astype(jnp.int32)
    own_at = jnp.concatenate([tile_rows[0, 0], tile_cols[0, 0], counts[0]])
    sib_at = lax.ppermute(own_at, "col", flip_core)

    def build(ready):
        own_tiles, ready = lax.optimization_barrier((tiles[0, 0], ready))
        sib_tiles = lax.ppermute(own_tiles, "col", flip_core)
        return build_dense(own_at, sib_at, meta, tiles[0, 0], sib_tiles, n_row, n_col)

    early, late, dense = gather_pieces(embedding.astype(jnp.bfloat16), n_row, n_col, build)
    total = embedding
    for layer in range(LAYERS):
        head = head_multiply(dense, early)
        theirs = tail_multiply(dense, head, late, 1, jnp.bfloat16)
        arrived = lax.ppermute(theirs, "col", flip_core)
        mine = tail_multiply(dense, head, late, 0, jnp.float32)
        pair = (mine + arrived.astype(jnp.float32)).astype(jnp.bfloat16)
        parts = lax.all_to_all(
            pair.reshape(n_col // 2, per_dev, width), "col", split_axis=0, concat_axis=0, axis_index_groups=groups
        )
        current = jnp.sum(parts.astype(jnp.float32), axis=0)
        total = total + current
        if layer + 1 < LAYERS:
            early, late, _ = gather_pieces(current.astype(jnp.bfloat16), n_row, n_col)
    return total / (LAYERS + 1.0)


def solution(mesh):
    return jax.shard_map(
        per_device,
        mesh=mesh,
        in_specs=(
            P(("row", "col"), None),
            P("row", "col", None, None, None),
            P("row", "col", None),
            P("row", "col", None),
            P("row", "col"),
        ),
        out_specs=P(("row", "col"), None),
        check_vma=False,
    )
```

```python
import jax
import jax.numpy as jnp
from jax import lax
from jax.experimental import pallas as pl
from jax.experimental.pallas import tpu as pltpu
from jax.sharding import PartitionSpec as P

LAYERS = 3
MIB = 1024 * 1024


def build_kernel(n_row, n_col, own_at_ref, sib_at_ref, meta_ref, own_ref, sib_ref, dense_ref, acc_ref):
    tile = own_ref.shape[1]
    slots = own_ref.shape[0]
    half = n_col // 2
    ring = n_row // 2
    my_row, my_col = meta_ref[0], meta_ref[1]
    core = my_col & 1
    acc_ref[...] = jnp.zeros_like(acc_ref)

    def add_tiles(at_ref, tiles_ref, sibling):
        def add_tile(k, carry):
            row, col = at_ref[k], at_ref[slots + k]
            row_at = ((row ^ my_col) & 1) * half + (row >> 1)
            ahead = ((col >> 1) + ring - (my_row >> 1)) & (ring - 1)
            away = jnp.where(core == 1, ahead, (ring - ahead) & (ring - 1))
            piece = jnp.maximum(2 * away - 1 + sibling, 0)
            late = 2 * ring - ring // 2
            near_at = jnp.where(piece < ring - 1, piece, late)
            far_at = jnp.where(piece < ring - 3, piece + ring - 1, piece + ring)
            col_at = jnp.where(((col ^ my_row) & 1) == 1, far_at, near_at)
            if sibling:
                keep = (away > 0) & (away < ring // 2)
            else:
                keep = away <= ring // 2

            @pl.when(keep)
            def _():
                at = (
                    pl.ds(pl.multiple_of(row_at * tile, tile), tile),
                    pl.ds(pl.multiple_of(col_at * tile, tile), tile),
                )
                acc_ref[at] += tiles_ref[k].astype(jnp.float32)

            return carry

        lax.fori_loop(0, at_ref[2 * slots], add_tile, 0)

    add_tiles(own_at_ref, own_ref, 0)
    add_tiles(sib_at_ref, sib_ref, 1)

    def emit(r, carry):
        at = pl.ds(pl.multiple_of(r * tile, tile), tile)
        dense_ref[at, :] = acc_ref[at, :].astype(jnp.bfloat16)
        return carry

    lax.fori_loop(0, dense_ref.shape[0] // tile, emit, 0)


def build_dense(own_at, sib_at, meta, own_tiles, sib_tiles, n_row, n_col):
    tile = own_tiles.shape[1]
    shape = (n_col * tile, n_row * tile)
    smem = pl.BlockSpec(memory_space=pltpu.SMEM)
    vmem = pl.BlockSpec(memory_space=pltpu.VMEM)

    def kernel(*refs):
        build_kernel(n_row, n_col, *refs)

    return pl.pallas_call(
        kernel,
        out_shape=jax.ShapeDtypeStruct(shape, jnp.bfloat16),
        in_specs=[smem, smem, smem, vmem, vmem],
        out_specs=vmem,
        scratch_shapes=[pltpu.VMEM(shape, jnp.float32)],
        compiler_params=pltpu.CompilerParams(vmem_limit_bytes=36 * MIB),
        cost_estimate=pl.CostEstimate(flops=shape[0] * shape[1], bytes_accessed=6 * shape[0] * shape[1], transcendentals=0),
        name="build_dense",
    )(own_at, sib_at, meta, own_tiles, sib_tiles)


def dot_rows(dense_ref, panel_ref, first, n_rows, step, store):
    depth = panel_ref.shape[0]
    lanes = dense_ref.shape[1] - depth if first[1] else 0

    def rows(i, carry):
        at = pl.multiple_of(i * step, step)
        store(at, jnp.dot(
            dense_ref[pl.ds(first[0] + at, step), lanes:lanes + depth],
            panel_ref[...],
            preferred_element_type=jnp.float32,
        ))
        return carry

    lax.fori_loop(0, n_rows // step, rows, 0)


def load_panel(panel_ref, refs):
    at = 0
    for ref in refs:
        rows = ref.shape[0]
        panel_ref[at:at + rows, :] = ref[...]
        at += rows


def head_multiply(dense, pieces):
    n_rows = dense.shape[0]
    depth = sum(piece.shape[0] for piece in pieces)
    width = pieces[0].shape[1]
    vmem = pl.BlockSpec(memory_space=pltpu.VMEM)

    def kernel(dense_ref, *refs):
        out_ref, panel_ref = refs[-2:]
        load_panel(panel_ref, refs[:-2])

        def store(at, value):
            out_ref[pl.ds(at, 512), :] = value

        dot_rows(dense_ref, panel_ref, (0, False), n_rows, 512, store)

    return pl.pallas_call(
        kernel,
        out_shape=jax.ShapeDtypeStruct((n_rows, width), jnp.float32),
        in_specs=[vmem] * (1 + len(pieces)),
        out_specs=vmem,
        scratch_shapes=[pltpu.VMEM((depth, width), jnp.bfloat16)],
        compiler_params=pltpu.CompilerParams(vmem_limit_bytes=24 * MIB),
        cost_estimate=pl.CostEstimate(
            flops=2 * n_rows * depth * width, bytes_accessed=2 * n_rows * depth, transcendentals=0
        ),
        name="head_multiply",
    )(dense, *pieces)


def tail_multiply(dense, head, pieces, half_index, dtype):
    n_rows = dense.shape[0] // 2
    depth = sum(piece.shape[0] for piece in pieces)
    width = pieces[0].shape[1]
    first = half_index * n_rows
    vmem = pl.BlockSpec(memory_space=pltpu.VMEM)

    def kernel(dense_ref, head_ref, *refs):
        out_ref, panel_ref = refs[-2:]
        load_panel(panel_ref, refs[:-2])

        def store(at, value):
            out_ref[pl.ds(at, 512), :] = (value + head_ref[pl.ds(first + at, 512), :]).astype(dtype)

        dot_rows(dense_ref, panel_ref, (first, True), n_rows, 512, store)

    return pl.pallas_call(
        kernel,
        out_shape=jax.ShapeDtypeStruct((n_rows, width), dtype),
        in_specs=[vmem] * (2 + len(pieces)),
        out_specs=vmem,
        scratch_shapes=[pltpu.VMEM((depth, width), jnp.bfloat16)],
        compiler_params=pltpu.CompilerParams(vmem_limit_bytes=24 * MIB),
        cost_estimate=pl.CostEstimate(
            flops=2 * n_rows * depth * width, bytes_accessed=2 * n_rows * depth, transcendentals=0
        ),
        name="tail_multiply",
    )(dense, head, *pieces)


def gather_pieces(own, n_row, n_col, build=None):
    ring = n_row // 2
    rows = own.shape[0]
    flip_x = [(i, i ^ 1) for i in range(n_row)]
    flip_core = [(j, j ^ 1) for j in range(n_col)]

    def onward(piece, by, name):
        pairs = []
        for i in range(n_row):
            for j in range(n_col):
                step = -by if j & 1 else by
                to = ((i >> 1) + step) % ring * 2 + (i & 1)
                pairs.append((i * n_col + j, to * n_col + j))
        with jax.named_scope(name):
            return lax.ppermute(piece, ("row", "col"), pairs)

    def over(piece, name):
        with jax.named_scope(name):
            return lax.ppermute(piece, "row", flip_x)

    def swap(piece):
        with jax.named_scope("core_swap"):
            return lax.ppermute(piece, "col", flip_core)

    sibling = swap(own)
    both = jnp.concatenate([own, sibling])
    one = onward(both, 1, "z_one")
    two = onward(both, 2, "z_two")
    if build is not None:
        three = onward(both, 3, "z_three")
        over_one = over(jnp.concatenate([own, one]), "x_one")
        over_two = over(two, "x_two")
        four = onward(three[:rows], 1, "z_four")
        over_three = over(three, "x_three")
        last, dense = lax.optimization_barrier((four, build(sibling)))
        over_four = over(last, "x_four")
        return [own, one, two, three, over_one, over_two], [four, over_three, over_four], dense
    two, over_own = lax.optimization_barrier((two, over(own, "x_own")))
    over_near = over(jnp.concatenate([one, two]), "x_near")
    three = onward(two, 1, "z_three")
    four = onward(two[:rows], 2, "z_four")
    far = jnp.concatenate([three, four])
    over_far = over(far, "x_far")
    return [own, one, two, three, over_own, over_near], [four, over_far], None


def per_device(embedding, tiles, tile_rows, tile_cols, counts):
    n_row = lax.axis_size("row")
    n_col = lax.axis_size("col")
    per_dev, width = embedding.shape
    flip_core = [(j, j ^ 1) for j in range(n_col)]
    groups = [list(range(core, n_col, 2)) for core in range(2)]

    meta = jnp.stack([lax.axis_index("row"), lax.axis_index("col")]).astype(jnp.int32)
    own_at = jnp.concatenate([tile_rows[0, 0], tile_cols[0, 0], counts[0]])
    with jax.named_scope("place_swap"):
        sib_at = lax.ppermute(own_at, "col", flip_core)

    def build(ready):
        own_tiles, ready = lax.optimization_barrier((tiles[0, 0], ready))
        with jax.named_scope("tile_swap"):
            sib_tiles = lax.ppermute(own_tiles, "col", flip_core)
        return build_dense(own_at, sib_at, meta, tiles[0, 0], sib_tiles, n_row, n_col)

    early, late, dense = gather_pieces(embedding.astype(jnp.bfloat16), n_row, n_col, build)
    total = embedding
    for layer in range(LAYERS):
        head = head_multiply(dense, early)
        theirs = tail_multiply(dense, head, late, 1, jnp.bfloat16)
        with jax.named_scope("partial_swap"):
            arrived = lax.ppermute(theirs, "col", flip_core)
        mine = tail_multiply(dense, head, late, 0, jnp.float32)
        pair = (mine + arrived.astype(jnp.float32)).astype(jnp.bfloat16)
        parts = lax.all_to_all(
            pair.reshape(n_col // 2, per_dev, width), "col", split_axis=0, concat_axis=0, axis_index_groups=groups
        )
        current = jnp.sum(parts.astype(jnp.float32), axis=0)
        total = total + current
        if layer + 1 < LAYERS:
            early, late, _ = gather_pieces(current.astype(jnp.bfloat16), n_row, n_col)
    return total / (LAYERS + 1.0)


def solution(mesh):
    return jax.shard_map(
        per_device,
        mesh=mesh,
        in_specs=(
            P(("row", "col"), None),
            P("row", "col", None, None, None),
            P("row", "col", None),
            P("row", "col", None),
            P("row", "col"),
        ),
        out_specs=P(("row", "col"), None),
        check_vma=False,
    )
```

```python
import jax
import jax.numpy as jnp
from jax import lax
from jax.experimental import pallas as pl
from jax.experimental.pallas import tpu as pltpu
from jax.sharding import PartitionSpec as P

LAYERS = 3
MIB = 1024 * 1024


def build_kernel(
    n_row, n_col, own_at_ref, sib_at_ref, meta_ref, own_ref, sib_ref, dense_ref, last_ref, before_ref, cell_ref
):
    tile = own_ref.shape[1]
    slots = own_ref.shape[0]
    half = n_col // 2
    ring = n_row // 2
    my_row, my_col = meta_ref[0], meta_ref[1]
    core = my_col & 1
    dense_ref[...] = jnp.zeros_like(dense_ref)

    def clear(cell, carry):
        last_ref[cell] = -1
        return carry

    lax.fori_loop(0, n_row * n_col, clear, 0)

    def add_tiles(at_ref, tiles_ref, sibling):
        count = at_ref[2 * slots]

        def link(k, carry):
            row, col = at_ref[k], at_ref[slots + k]
            row_at = ((row ^ my_col) & 1) * half + (row >> 1)
            ahead = ((col >> 1) + ring - (my_row >> 1)) & (ring - 1)
            away = jnp.where(core == 1, ahead, (ring - ahead) & (ring - 1))
            piece = jnp.maximum(2 * away - 1 + sibling, 0)
            col_at = ((col ^ my_row) & 1) * ring + piece
            if sibling:
                keep = (away > 0) & (away < ring // 2)
            else:
                keep = away <= ring // 2
            cell = row_at * n_row + col_at
            cell_ref[k] = jnp.where(keep, cell, -1)

            @pl.when(keep)
            def _():
                before_ref[k] = last_ref[cell]
                last_ref[cell] = k

            return carry

        lax.fori_loop(0, count, link, 0)

        def write(k, carry):
            cell = jnp.maximum(cell_ref[k], 0)

            @pl.when((cell_ref[k] >= 0) & (last_ref[cell] == k))
            def _():
                def add(state):
                    j, value = state
                    return before_ref[j], value + tiles_ref[j].astype(jnp.float32)

                start = (before_ref[k], tiles_ref[k].astype(jnp.float32))
                _, value = lax.while_loop(lambda state: state[0] >= 0, add, start)
                at = (
                    pl.ds(pl.multiple_of((cell // n_row) * tile, tile), tile),
                    pl.ds(pl.multiple_of((cell % n_row) * tile, tile), tile),
                )
                dense_ref[at] = value.astype(jnp.bfloat16)

            return carry

        lax.fori_loop(0, count, write, 0)

    add_tiles(own_at_ref, own_ref, 0)
    add_tiles(sib_at_ref, sib_ref, 1)


def build_dense(own_at, sib_at, meta, own_tiles, sib_tiles, n_row, n_col):
    tile = own_tiles.shape[1]
    shape = (n_col * tile, n_row * tile)
    smem = pl.BlockSpec(memory_space=pltpu.SMEM)
    vmem = pl.BlockSpec(memory_space=pltpu.VMEM)

    def kernel(*refs):
        build_kernel(n_row, n_col, *refs)

    return pl.pallas_call(
        kernel,
        out_shape=jax.ShapeDtypeStruct(shape, jnp.bfloat16),
        in_specs=[smem, smem, smem, vmem, vmem],
        out_specs=vmem,
        scratch_shapes=[
            pltpu.SMEM((n_row * n_col,), jnp.int32),
            pltpu.SMEM((own_tiles.shape[0],), jnp.int32),
            pltpu.SMEM((own_tiles.shape[0],), jnp.int32),
        ],
        compiler_params=pltpu.CompilerParams(vmem_limit_bytes=36 * MIB),
        cost_estimate=pl.CostEstimate(flops=shape[0] * shape[1], bytes_accessed=6 * shape[0] * shape[1], transcendentals=0),
        name="build_dense",
    )(own_at, sib_at, meta, own_tiles, sib_tiles)


def dot_rows(dense_ref, panel_ref, first, n_rows, step, store):
    depth = panel_ref.shape[0]
    lanes = dense_ref.shape[1] - depth if first[1] else 0

    def rows(i, carry):
        at = pl.multiple_of(i * step, step)
        store(at, jnp.dot(
            dense_ref[pl.ds(first[0] + at, step), lanes:lanes + depth],
            panel_ref[...],
            preferred_element_type=jnp.float32,
        ))
        return carry

    lax.fori_loop(0, n_rows // step, rows, 0)


def load_panel(panel_ref, refs):
    at = 0
    for ref in refs:
        rows = ref.shape[0]
        panel_ref[at:at + rows, :] = ref[...]
        at += rows


def head_multiply(dense, pieces):
    n_rows = dense.shape[0]
    depth = sum(piece.shape[0] for piece in pieces)
    width = pieces[0].shape[1]
    vmem = pl.BlockSpec(memory_space=pltpu.VMEM)

    def kernel(dense_ref, *refs):
        out_ref, panel_ref = refs[-2:]
        load_panel(panel_ref, refs[:-2])

        def store(at, value):
            out_ref[pl.ds(at, 512), :] = value

        dot_rows(dense_ref, panel_ref, (0, False), n_rows, 512, store)

    return pl.pallas_call(
        kernel,
        out_shape=jax.ShapeDtypeStruct((n_rows, width), jnp.float32),
        in_specs=[vmem] * (1 + len(pieces)),
        out_specs=vmem,
        scratch_shapes=[pltpu.VMEM((depth, width), jnp.bfloat16)],
        compiler_params=pltpu.CompilerParams(vmem_limit_bytes=24 * MIB),
        cost_estimate=pl.CostEstimate(
            flops=2 * n_rows * depth * width, bytes_accessed=2 * n_rows * depth, transcendentals=0
        ),
        name="head_multiply",
    )(dense, *pieces)


def tail_multiply(dense, head, pieces, half_index, dtype):
    n_rows = dense.shape[0] // 2
    depth = sum(piece.shape[0] for piece in pieces)
    width = pieces[0].shape[1]
    first = half_index * n_rows
    vmem = pl.BlockSpec(memory_space=pltpu.VMEM)

    def kernel(dense_ref, head_ref, *refs):
        out_ref, panel_ref = refs[-2:]
        load_panel(panel_ref, refs[:-2])

        def store(at, value):
            out_ref[pl.ds(at, 512), :] = (value + head_ref[pl.ds(first + at, 512), :]).astype(dtype)

        dot_rows(dense_ref, panel_ref, (first, True), n_rows, 512, store)

    return pl.pallas_call(
        kernel,
        out_shape=jax.ShapeDtypeStruct((n_rows, width), dtype),
        in_specs=[vmem] * (2 + len(pieces)),
        out_specs=vmem,
        scratch_shapes=[pltpu.VMEM((depth, width), jnp.bfloat16)],
        compiler_params=pltpu.CompilerParams(vmem_limit_bytes=24 * MIB),
        cost_estimate=pl.CostEstimate(
            flops=2 * n_rows * depth * width, bytes_accessed=2 * n_rows * depth, transcendentals=0
        ),
        name="tail_multiply",
    )(dense, head, *pieces)


def gather_pieces(own, n_row, n_col, build=None):
    ring = n_row // 2
    rows = own.shape[0]
    flip_x = [(i, i ^ 1) for i in range(n_row)]
    flip_core = [(j, j ^ 1) for j in range(n_col)]

    def onward(piece, by):
        pairs = []
        for i in range(n_row):
            for j in range(n_col):
                step = -by if j & 1 else by
                to = ((i >> 1) + step) % ring * 2 + (i & 1)
                pairs.append((i * n_col + j, to * n_col + j))
        return lax.ppermute(piece, ("row", "col"), pairs)

    def over(piece):
        return lax.ppermute(piece, "row", flip_x)

    sibling = lax.ppermute(own, "col", flip_core)
    both = jnp.concatenate([own, sibling])
    one = onward(both, 1)
    two = onward(both, 2)
    two, over_own = lax.optimization_barrier((two, over(own)))
    dense = None
    if build is not None:
        two, dense = lax.optimization_barrier((two, build(sibling)))
    over_near = over(jnp.concatenate([one, two]))
    three = onward(two, 1)
    four = onward(two[:rows], 2)
    far = jnp.concatenate([three, four])
    return [own, one, two, far, over_own, over_near], [over(far)], dense


def per_device(embedding, tiles, tile_rows, tile_cols, counts):
    n_row = lax.axis_size("row")
    n_col = lax.axis_size("col")
    per_dev, width = embedding.shape
    flip_core = [(j, j ^ 1) for j in range(n_col)]
    groups = [list(range(core, n_col, 2)) for core in range(2)]

    meta = jnp.stack([lax.axis_index("row"), lax.axis_index("col")]).astype(jnp.int32)
    own_at = jnp.concatenate([tile_rows[0, 0], tile_cols[0, 0], counts[0]])
    sib_at = lax.ppermute(own_at, "col", flip_core)

    def build(ready):
        own_tiles, ready = lax.optimization_barrier((tiles[0, 0], ready))
        sib_tiles = lax.ppermute(own_tiles, "col", flip_core)
        return build_dense(own_at, sib_at, meta, tiles[0, 0], sib_tiles, n_row, n_col)

    early, late, dense = gather_pieces(embedding.astype(jnp.bfloat16), n_row, n_col, build)
    total = embedding
    for layer in range(LAYERS):
        head = head_multiply(dense, early)
        theirs = tail_multiply(dense, head, late, 1, jnp.bfloat16)
        arrived = lax.ppermute(theirs, "col", flip_core)
        mine = tail_multiply(dense, head, late, 0, jnp.float32)
        pair = (mine + arrived.astype(jnp.float32)).astype(jnp.bfloat16)
        parts = lax.all_to_all(
            pair.reshape(n_col // 2, per_dev, width), "col", split_axis=0, concat_axis=0, axis_index_groups=groups
        )
        current = jnp.sum(parts.astype(jnp.float32), axis=0)
        total = total + current
        if layer + 1 < LAYERS:
            early, late, _ = gather_pieces(current.astype(jnp.bfloat16), n_row, n_col)
    return total / (LAYERS + 1.0)


def solution(mesh):
    return jax.shard_map(
        per_device,
        mesh=mesh,
        in_specs=(
            P(("row", "col"), None),
            P("row", "col", None, None, None),
            P("row", "col", None),
            P("row", "col", None),
            P("row", "col"),
        ),
        out_specs=P(("row", "col"), None),
        check_vma=False,
    )
```

```python
import jax
import jax.numpy as jnp
from jax import lax
from jax.experimental import pallas as pl
from jax.experimental.pallas import tpu as pltpu
from jax.sharding import PartitionSpec as P

LAYERS = 3
MIB = 1024 * 1024


def build_kernel(n_row, n_col, own_at_ref, sib_at_ref, meta_ref, own_ref, sib_ref, dense_ref, acc_ref):
    tile = own_ref.shape[1]
    slots = own_ref.shape[0]
    half = n_col // 2
    ring = n_row // 2
    my_row, my_col = meta_ref[0], meta_ref[1]
    core = my_col & 1
    acc_ref[...] = jnp.zeros_like(acc_ref)

    def add_tiles(at_ref, tiles_ref, sibling):
        def add_tile(k, carry):
            row, col = at_ref[k], at_ref[slots + k]
            row_at = ((row ^ my_col) & 1) * half + (row >> 1)
            ahead = ((col >> 1) + ring - (my_row >> 1)) & (ring - 1)
            away = jnp.where(core == 1, ahead, (ring - ahead) & (ring - 1))
            piece = jnp.maximum(2 * away - 1 + sibling, 0)
            col_at = ((col ^ my_row) & 1) * ring + piece
            if sibling:
                keep = (away > 0) & (away < ring // 2)
            else:
                keep = away <= ring // 2

            @pl.when(keep)
            def _():
                at = (
                    pl.ds(pl.multiple_of(row_at * tile, tile), tile),
                    pl.ds(pl.multiple_of(col_at * tile, tile), tile),
                )
                acc_ref[at] += tiles_ref[k].astype(jnp.float32)

            return carry

        lax.fori_loop(0, at_ref[2 * slots], add_tile, 0)

    add_tiles(own_at_ref, own_ref, 0)
    add_tiles(sib_at_ref, sib_ref, 1)

    def emit(r, carry):
        at = pl.ds(pl.multiple_of(r * tile, tile), tile)
        dense_ref[at, :] = acc_ref[at, :].astype(jnp.bfloat16)
        return carry

    lax.fori_loop(0, dense_ref.shape[0] // tile, emit, 0)


def build_dense(own_at, sib_at, meta, own_tiles, sib_tiles, n_row, n_col):
    tile = own_tiles.shape[1]
    shape = (n_col * tile, n_row * tile)
    smem = pl.BlockSpec(memory_space=pltpu.SMEM)
    vmem = pl.BlockSpec(memory_space=pltpu.VMEM)

    def kernel(*refs):
        build_kernel(n_row, n_col, *refs)

    return pl.pallas_call(
        kernel,
        out_shape=jax.ShapeDtypeStruct(shape, jnp.bfloat16),
        in_specs=[smem, smem, smem, vmem, vmem],
        out_specs=vmem,
        scratch_shapes=[pltpu.VMEM(shape, jnp.float32)],
        compiler_params=pltpu.CompilerParams(vmem_limit_bytes=36 * MIB),
        cost_estimate=pl.CostEstimate(flops=shape[0] * shape[1], bytes_accessed=6 * shape[0] * shape[1], transcendentals=0),
        name="build_dense",
    )(own_at, sib_at, meta, own_tiles, sib_tiles)


def dot_rows(dense_ref, panel_ref, first, n_rows, step, store):
    depth = panel_ref.shape[0]
    lanes = dense_ref.shape[1] - depth if first[1] else 0

    def rows(i, carry):
        at = pl.multiple_of(i * step, step)
        store(at, jnp.dot(
            dense_ref[pl.ds(first[0] + at, step), lanes:lanes + depth],
            panel_ref[...],
            preferred_element_type=jnp.float32,
        ))
        return carry

    lax.fori_loop(0, n_rows // step, rows, 0)


def load_panel(panel_ref, refs):
    at = 0
    for ref in refs:
        rows = ref.shape[0]
        panel_ref[at:at + rows, :] = ref[...]
        at += rows


def head_multiply(dense, pieces):
    n_rows = dense.shape[0]
    depth = sum(piece.shape[0] for piece in pieces)
    width = pieces[0].shape[1]
    vmem = pl.BlockSpec(memory_space=pltpu.VMEM)

    def kernel(dense_ref, *refs):
        out_ref, panel_ref = refs[-2:]
        load_panel(panel_ref, refs[:-2])

        def store(at, value):
            out_ref[pl.ds(at, 512), :] = value

        dot_rows(dense_ref, panel_ref, (0, False), n_rows, 512, store)

    return pl.pallas_call(
        kernel,
        out_shape=jax.ShapeDtypeStruct((n_rows, width), jnp.float32),
        in_specs=[vmem] * (1 + len(pieces)),
        out_specs=vmem,
        scratch_shapes=[pltpu.VMEM((depth, width), jnp.bfloat16)],
        compiler_params=pltpu.CompilerParams(vmem_limit_bytes=24 * MIB),
        cost_estimate=pl.CostEstimate(
            flops=2 * n_rows * depth * width, bytes_accessed=2 * n_rows * depth, transcendentals=0
        ),
        name="head_multiply",
    )(dense, *pieces)


def tail_multiply(dense, head, pieces, half_index, dtype):
    n_rows = dense.shape[0] // 2
    depth = sum(piece.shape[0] for piece in pieces)
    width = pieces[0].shape[1]
    first = half_index * n_rows
    vmem = pl.BlockSpec(memory_space=pltpu.VMEM)

    def kernel(dense_ref, head_ref, *refs):
        out_ref, panel_ref = refs[-2:]
        load_panel(panel_ref, refs[:-2])

        def store(at, value):
            out_ref[pl.ds(at, 512), :] = (value + head_ref[pl.ds(first + at, 512), :]).astype(dtype)

        dot_rows(dense_ref, panel_ref, (first, True), n_rows, 512, store)

    return pl.pallas_call(
        kernel,
        out_shape=jax.ShapeDtypeStruct((n_rows, width), dtype),
        in_specs=[vmem] * (2 + len(pieces)),
        out_specs=vmem,
        scratch_shapes=[pltpu.VMEM((depth, width), jnp.bfloat16)],
        compiler_params=pltpu.CompilerParams(vmem_limit_bytes=24 * MIB),
        cost_estimate=pl.CostEstimate(
            flops=2 * n_rows * depth * width, bytes_accessed=2 * n_rows * depth, transcendentals=0
        ),
        name="tail_multiply",
    )(dense, head, *pieces)


def gather_pieces(own, n_row, n_col, build=None):
    ring = n_row // 2
    rows = own.shape[0]
    flip_x = [(i, i ^ 1) for i in range(n_row)]
    flip_core = [(j, j ^ 1) for j in range(n_col)]

    def onward(piece, by):
        pairs = []
        for i in range(n_row):
            for j in range(n_col):
                step = -by if j & 1 else by
                to = ((i >> 1) + step) % ring * 2 + (i & 1)
                pairs.append((i * n_col + j, to * n_col + j))
        return lax.ppermute(piece, ("row", "col"), pairs)

    def over(piece, name):
        with jax.named_scope(name):
            return lax.ppermute(piece, "row", flip_x)

    sibling = lax.ppermute(own, "col", flip_core)
    both = jnp.concatenate([own, sibling])
    with jax.named_scope("z_one"):
        one = onward(both, 1)
    with jax.named_scope("z_two"):
        two = onward(both, 2)
    if build is not None:
        with jax.named_scope("z_three"):
            three = onward(both, 3)
        over_one = over(jnp.concatenate([own, one]), "x_one")
        over_two = over(two, "x_two")
        with jax.named_scope("z_four"):
            four = onward(three[:rows], 1)
        over_three = over(three, "x_three")
        last, dense = lax.optimization_barrier((four, build(sibling)))
        over_four = over(last, "x_four")
        return [own, one, two, three, four, over_one, over_two], [over_three, over_four], dense
    one, over_own = lax.optimization_barrier((one, over(own, "x_own")))
    over_near = over(jnp.concatenate([one, two]), "x_near")
    with jax.named_scope("z_three"):
        three = onward(two, 1)
    with jax.named_scope("z_four"):
        four = onward(two[:rows], 2)
    far = jnp.concatenate([three, four])
    return [own, one, two, far, over_own, over_near], [over(far, "x_far")], None


def per_device(embedding, tiles, tile_rows, tile_cols, counts):
    n_row = lax.axis_size("row")
    n_col = lax.axis_size("col")
    per_dev, width = embedding.shape
    flip_core = [(j, j ^ 1) for j in range(n_col)]
    groups = [list(range(core, n_col, 2)) for core in range(2)]

    meta = jnp.stack([lax.axis_index("row"), lax.axis_index("col")]).astype(jnp.int32)
    own_at = jnp.concatenate([tile_rows[0, 0], tile_cols[0, 0], counts[0]])
    sib_at = lax.ppermute(own_at, "col", flip_core)

    def build(ready):
        own_tiles, ready = lax.optimization_barrier((tiles[0, 0], ready))
        sib_tiles = lax.ppermute(own_tiles, "col", flip_core)
        return build_dense(own_at, sib_at, meta, tiles[0, 0], sib_tiles, n_row, n_col)

    early, late, dense = gather_pieces(embedding.astype(jnp.bfloat16), n_row, n_col, build)
    total = embedding
    for layer in range(LAYERS):
        head = head_multiply(dense, early)
        theirs = tail_multiply(dense, head, late, 1, jnp.bfloat16)
        arrived = lax.ppermute(theirs, "col", flip_core)
        mine = tail_multiply(dense, head, late, 0, jnp.float32)
        pair = (mine + arrived.astype(jnp.float32)).astype(jnp.bfloat16)
        parts = lax.all_to_all(
            pair.reshape(n_col // 2, per_dev, width), "col", split_axis=0, concat_axis=0, axis_index_groups=groups
        )
        current = jnp.sum(parts.astype(jnp.float32), axis=0)
        total = total + current
        if layer + 1 < LAYERS:
            early, late, _ = gather_pieces(current.astype(jnp.bfloat16), n_row, n_col)
    return total / (LAYERS + 1.0)


def solution(mesh):
    return jax.shard_map(
        per_device,
        mesh=mesh,
        in_specs=(
            P(("row", "col"), None),
            P("row", "col", None, None, None),
            P("row", "col", None),
            P("row", "col", None),
            P("row", "col"),
        ),
        out_specs=P(("row", "col"), None),
        check_vma=False,
    )
```

```python
import jax
import jax.numpy as jnp
from jax import lax
from jax.experimental import pallas as pl
from jax.experimental.pallas import tpu as pltpu
from jax.sharding import PartitionSpec as P

LAYERS = 3
MIB = 1024 * 1024


def build_kernel(n_row, n_col, own_at_ref, sib_at_ref, meta_ref, own_ref, sib_ref, dense_ref, acc_ref):
    tile = own_ref.shape[1]
    slots = own_ref.shape[0]
    half = n_col // 2
    ring = n_row // 2
    my_row, my_col = meta_ref[0], meta_ref[1]
    core = my_col & 1
    acc_ref[...] = jnp.zeros_like(acc_ref)

    def add_tiles(at_ref, tiles_ref, sibling):
        def add_tile(k, carry):
            row, col = at_ref[k], at_ref[slots + k]
            row_at = ((row ^ my_col) & 1) * half + (row >> 1)
            ahead = ((col >> 1) + ring - (my_row >> 1)) & (ring - 1)
            away = jnp.where(core == 1, ahead, (ring - ahead) & (ring - 1))
            piece = jnp.maximum(2 * away - 1 + sibling, 0)
            col_at = ((col ^ my_row) & 1) * ring + piece
            if sibling:
                keep = (away > 0) & (away < ring // 2)
            else:
                keep = away <= ring // 2

            @pl.when(keep)
            def _():
                at = (
                    pl.ds(pl.multiple_of(row_at * tile, tile), tile),
                    pl.ds(pl.multiple_of(col_at * tile, tile), tile),
                )
                acc_ref[at] += tiles_ref[k].astype(jnp.float32)

            return carry

        lax.fori_loop(0, at_ref[2 * slots], add_tile, 0)

    add_tiles(own_at_ref, own_ref, 0)
    add_tiles(sib_at_ref, sib_ref, 1)

    def emit(r, carry):
        at = pl.ds(pl.multiple_of(r * tile, tile), tile)
        dense_ref[at, :] = acc_ref[at, :].astype(jnp.bfloat16)
        return carry

    lax.fori_loop(0, dense_ref.shape[0] // tile, emit, 0)


def build_dense(own_at, sib_at, meta, own_tiles, sib_tiles, n_row, n_col):
    tile = own_tiles.shape[1]
    shape = (n_col * tile, n_row * tile)
    smem = pl.BlockSpec(memory_space=pltpu.SMEM)
    vmem = pl.BlockSpec(memory_space=pltpu.VMEM)

    def kernel(*refs):
        build_kernel(n_row, n_col, *refs)

    return pl.pallas_call(
        kernel,
        out_shape=jax.ShapeDtypeStruct(shape, jnp.bfloat16),
        in_specs=[smem, smem, smem, vmem, vmem],
        out_specs=vmem,
        scratch_shapes=[pltpu.VMEM(shape, jnp.float32)],
        compiler_params=pltpu.CompilerParams(vmem_limit_bytes=36 * MIB),
        cost_estimate=pl.CostEstimate(flops=shape[0] * shape[1], bytes_accessed=6 * shape[0] * shape[1], transcendentals=0),
        name="build_dense",
    )(own_at, sib_at, meta, own_tiles, sib_tiles)


def dot_rows(dense_ref, panel_ref, first, n_rows, step, store):
    depth = panel_ref.shape[0]
    lanes = dense_ref.shape[1] - depth if first[1] else 0

    def rows(i, carry):
        at = pl.multiple_of(i * step, step)
        store(at, jnp.dot(
            dense_ref[pl.ds(first[0] + at, step), lanes:lanes + depth],
            panel_ref[...],
            preferred_element_type=jnp.float32,
        ))
        return carry

    lax.fori_loop(0, n_rows // step, rows, 0)


def load_panel(panel_ref, refs):
    at = 0
    for ref in refs:
        rows = ref.shape[0]
        panel_ref[at:at + rows, :] = ref[...]
        at += rows


def head_multiply(dense, pieces):
    n_rows = dense.shape[0]
    depth = sum(piece.shape[0] for piece in pieces)
    width = pieces[0].shape[1]
    vmem = pl.BlockSpec(memory_space=pltpu.VMEM)

    def kernel(dense_ref, *refs):
        out_ref, panel_ref = refs[-2:]
        load_panel(panel_ref, refs[:-2])

        def store(at, value):
            out_ref[pl.ds(at, 512), :] = value

        dot_rows(dense_ref, panel_ref, (0, False), n_rows, 512, store)

    return pl.pallas_call(
        kernel,
        out_shape=jax.ShapeDtypeStruct((n_rows, width), jnp.float32),
        in_specs=[vmem] * (1 + len(pieces)),
        out_specs=vmem,
        scratch_shapes=[pltpu.VMEM((depth, width), jnp.bfloat16)],
        compiler_params=pltpu.CompilerParams(vmem_limit_bytes=24 * MIB),
        cost_estimate=pl.CostEstimate(
            flops=2 * n_rows * depth * width, bytes_accessed=2 * n_rows * depth, transcendentals=0
        ),
        name="head_multiply",
    )(dense, *pieces)


def tail_multiply(dense, head, pieces, half_index, dtype):
    n_rows = dense.shape[0] // 2
    depth = sum(piece.shape[0] for piece in pieces)
    width = pieces[0].shape[1]
    first = half_index * n_rows
    vmem = pl.BlockSpec(memory_space=pltpu.VMEM)

    def kernel(dense_ref, head_ref, *refs):
        out_ref, panel_ref = refs[-2:]
        load_panel(panel_ref, refs[:-2])

        def store(at, value):
            out_ref[pl.ds(at, 512), :] = (value + head_ref[pl.ds(first + at, 512), :]).astype(dtype)

        dot_rows(dense_ref, panel_ref, (first, True), n_rows, 512, store)

    return pl.pallas_call(
        kernel,
        out_shape=jax.ShapeDtypeStruct((n_rows, width), dtype),
        in_specs=[vmem] * (2 + len(pieces)),
        out_specs=vmem,
        scratch_shapes=[pltpu.VMEM((depth, width), jnp.bfloat16)],
        compiler_params=pltpu.CompilerParams(vmem_limit_bytes=24 * MIB),
        cost_estimate=pl.CostEstimate(
            flops=2 * n_rows * depth * width, bytes_accessed=2 * n_rows * depth, transcendentals=0
        ),
        name="tail_multiply",
    )(dense, head, *pieces)


def gather_pieces(own, n_row, n_col, build=None):
    ring = n_row // 2
    rows = own.shape[0]
    flip_x = [(i, i ^ 1) for i in range(n_row)]
    flip_core = [(j, j ^ 1) for j in range(n_col)]

    def onward(piece, by):
        pairs = []
        for i in range(n_row):
            for j in range(n_col):
                step = -by if j & 1 else by
                to = ((i >> 1) + step) % ring * 2 + (i & 1)
                pairs.append((i * n_col + j, to * n_col + j))
        return lax.ppermute(piece, ("row", "col"), pairs)

    def over(piece, name):
        with jax.named_scope(name):
            return lax.ppermute(piece, "row", flip_x)

    sibling = lax.ppermute(own, "col", flip_core)
    both = jnp.concatenate([own, sibling])
    with jax.named_scope("z_one"):
        one = onward(both, 1)
    with jax.named_scope("z_two"):
        two = onward(both, 2)
    if build is not None:
        with jax.named_scope("z_three"):
            three = onward(both, 3)
        over_one = over(jnp.concatenate([own, one]), "x_one")
        over_two = over(two, "x_two")
        with jax.named_scope("z_four"):
            four = onward(three[:rows], 1)
        over_three = over(three, "x_three")
        last, dense = lax.optimization_barrier((four, build(sibling)))
        over_four = over(last, "x_four")
        return [own, one, two, three, four, over_one, over_two], [over_three, over_four], dense
    two, over_own = lax.optimization_barrier((two, over(own, "x_own")))
    over_near = over(jnp.concatenate([one, two]), "x_near")
    with jax.named_scope("z_three"):
        three = onward(two, 1)
    with jax.named_scope("z_four"):
        four = onward(two[:rows], 2)
    far = jnp.concatenate([three, four])
    return [own, one, two, far, over_own, over_near], [over(far, "x_far")], None


def per_device(embedding, tiles, tile_rows, tile_cols, counts):
    n_row = lax.axis_size("row")
    n_col = lax.axis_size("col")
    per_dev, width = embedding.shape
    flip_core = [(j, j ^ 1) for j in range(n_col)]
    groups = [list(range(core, n_col, 2)) for core in range(2)]

    meta = jnp.stack([lax.axis_index("row"), lax.axis_index("col")]).astype(jnp.int32)
    own_at = jnp.concatenate([tile_rows[0, 0], tile_cols[0, 0], counts[0]])
    sib_at = lax.ppermute(own_at, "col", flip_core)

    def build(ready):
        own_tiles, ready = lax.optimization_barrier((tiles[0, 0], ready))
        sib_tiles = lax.ppermute(own_tiles, "col", flip_core)
        return build_dense(own_at, sib_at, meta, tiles[0, 0], sib_tiles, n_row, n_col)

    early, late, dense = gather_pieces(embedding.astype(jnp.bfloat16), n_row, n_col, build)
    total = embedding
    for layer in range(LAYERS):
        head = head_multiply(dense, early)
        theirs = tail_multiply(dense, head, late, 1, jnp.bfloat16)
        arrived = lax.ppermute(theirs, "col", flip_core)
        mine = tail_multiply(dense, head, late, 0, jnp.float32)
        pair = (mine + arrived.astype(jnp.float32)).astype(jnp.bfloat16)
        parts = lax.all_to_all(
            pair.reshape(n_col // 2, per_dev, width), "col", split_axis=0, concat_axis=0, axis_index_groups=groups
        )
        current = jnp.sum(parts.astype(jnp.float32), axis=0)
        total = total + current
        if layer + 1 < LAYERS:
            early, late, _ = gather_pieces(current.astype(jnp.bfloat16), n_row, n_col)
    return total / (LAYERS + 1.0)


def solution(mesh):
    return jax.shard_map(
        per_device,
        mesh=mesh,
        in_specs=(
            P(("row", "col"), None),
            P("row", "col", None, None, None),
            P("row", "col", None),
            P("row", "col", None),
            P("row", "col"),
        ),
        out_specs=P(("row", "col"), None),
        check_vma=False,
    )
```

```python
import jax
import jax.numpy as jnp
from jax import lax
from jax.experimental import pallas as pl
from jax.experimental.pallas import tpu as pltpu
from jax.sharding import PartitionSpec as P

LAYERS = 3
MIB = 1024 * 1024


def build_kernel(n_row, n_col, own_at_ref, sib_at_ref, meta_ref, own_ref, sib_ref, dense_ref, acc_ref):
    tile = own_ref.shape[1]
    slots = own_ref.shape[0]
    half = n_col // 2
    ring = n_row // 2
    my_row, my_col = meta_ref[0], meta_ref[1]
    core = my_col & 1
    acc_ref[...] = jnp.zeros_like(acc_ref)

    def add_tiles(at_ref, tiles_ref, sibling):
        def add_tile(k, carry):
            row, col = at_ref[k], at_ref[slots + k]
            row_at = ((row ^ my_col) & 1) * half + (row >> 1)
            ahead = ((col >> 1) + ring - (my_row >> 1)) & (ring - 1)
            away = jnp.where(core == 1, ahead, (ring - ahead) & (ring - 1))
            piece = jnp.maximum(2 * away - 1 + sibling, 0)
            col_at = ((col ^ my_row) & 1) * ring + piece
            if sibling:
                keep = (away > 0) & (away < ring // 2)
            else:
                keep = away <= ring // 2

            @pl.when(keep)
            def _():
                at = (
                    pl.ds(pl.multiple_of(row_at * tile, tile), tile),
                    pl.ds(pl.multiple_of(col_at * tile, tile), tile),
                )
                acc_ref[at] += tiles_ref[k].astype(jnp.float32)

            return carry

        lax.fori_loop(0, at_ref[2 * slots], add_tile, 0)

    add_tiles(own_at_ref, own_ref, 0)
    add_tiles(sib_at_ref, sib_ref, 1)

    def emit(r, carry):
        at = pl.ds(pl.multiple_of(r * tile, tile), tile)
        dense_ref[at, :] = acc_ref[at, :].astype(jnp.bfloat16)
        return carry

    lax.fori_loop(0, dense_ref.shape[0] // tile, emit, 0)


def build_dense(own_at, sib_at, meta, own_tiles, sib_tiles, n_row, n_col):
    tile = own_tiles.shape[1]
    shape = (n_col * tile, n_row * tile)
    smem = pl.BlockSpec(memory_space=pltpu.SMEM)
    vmem = pl.BlockSpec(memory_space=pltpu.VMEM)

    def kernel(*refs):
        build_kernel(n_row, n_col, *refs)

    return pl.pallas_call(
        kernel,
        out_shape=jax.ShapeDtypeStruct(shape, jnp.bfloat16),
        in_specs=[smem, smem, smem, vmem, vmem],
        out_specs=vmem,
        scratch_shapes=[pltpu.VMEM(shape, jnp.float32)],
        compiler_params=pltpu.CompilerParams(vmem_limit_bytes=36 * MIB),
        cost_estimate=pl.CostEstimate(flops=shape[0] * shape[1], bytes_accessed=6 * shape[0] * shape[1], transcendentals=0),
        name="build_dense",
    )(own_at, sib_at, meta, own_tiles, sib_tiles)


def dot_rows(dense_ref, panel_ref, first, n_rows, step, store):
    depth = panel_ref.shape[0]
    lanes = dense_ref.shape[1] - depth if first[1] else 0

    def rows(i, carry):
        at = pl.multiple_of(i * step, step)
        store(at, jnp.dot(
            dense_ref[pl.ds(first[0] + at, step), lanes:lanes + depth],
            panel_ref[...],
            preferred_element_type=jnp.float32,
        ))
        return carry

    lax.fori_loop(0, n_rows // step, rows, 0)


def load_panel(panel_ref, refs):
    at = 0
    for ref in refs:
        rows = ref.shape[0]
        panel_ref[at:at + rows, :] = ref[...]
        at += rows


def head_multiply(dense, pieces):
    n_rows = dense.shape[0]
    depth = sum(piece.shape[0] for piece in pieces)
    width = pieces[0].shape[1]
    vmem = pl.BlockSpec(memory_space=pltpu.VMEM)

    def kernel(dense_ref, *refs):
        out_ref, panel_ref = refs[-2:]
        load_panel(panel_ref, refs[:-2])

        def store(at, value):
            out_ref[pl.ds(at, 512), :] = value

        dot_rows(dense_ref, panel_ref, (0, False), n_rows, 512, store)

    return pl.pallas_call(
        kernel,
        out_shape=jax.ShapeDtypeStruct((n_rows, width), jnp.float32),
        in_specs=[vmem] * (1 + len(pieces)),
        out_specs=vmem,
        scratch_shapes=[pltpu.VMEM((depth, width), jnp.bfloat16)],
        compiler_params=pltpu.CompilerParams(vmem_limit_bytes=24 * MIB),
        cost_estimate=pl.CostEstimate(
            flops=2 * n_rows * depth * width, bytes_accessed=2 * n_rows * depth, transcendentals=0
        ),
        name="head_multiply",
    )(dense, *pieces)


def tail_multiply(dense, head, pieces, half_index, dtype):
    n_rows = dense.shape[0] // 2
    depth = sum(piece.shape[0] for piece in pieces)
    width = pieces[0].shape[1]
    first = half_index * n_rows
    vmem = pl.BlockSpec(memory_space=pltpu.VMEM)

    def kernel(dense_ref, head_ref, *refs):
        out_ref, panel_ref = refs[-2:]
        load_panel(panel_ref, refs[:-2])

        def store(at, value):
            out_ref[pl.ds(at, 512), :] = (value + head_ref[pl.ds(first + at, 512), :]).astype(dtype)

        dot_rows(dense_ref, panel_ref, (first, True), n_rows, 512, store)

    return pl.pallas_call(
        kernel,
        out_shape=jax.ShapeDtypeStruct((n_rows, width), dtype),
        in_specs=[vmem] * (2 + len(pieces)),
        out_specs=vmem,
        scratch_shapes=[pltpu.VMEM((depth, width), jnp.bfloat16)],
        compiler_params=pltpu.CompilerParams(vmem_limit_bytes=24 * MIB),
        cost_estimate=pl.CostEstimate(
            flops=2 * n_rows * depth * width, bytes_accessed=2 * n_rows * depth, transcendentals=0
        ),
        name="tail_multiply",
    )(dense, head, *pieces)


def gather_pieces(own, n_row, n_col, build=None):
    ring = n_row // 2
    rows = own.shape[0]
    flip_x = [(i, i ^ 1) for i in range(n_row)]
    flip_core = [(j, j ^ 1) for j in range(n_col)]

    def onward(piece, by):
        pairs = []
        for i in range(n_row):
            for j in range(n_col):
                step = -by if j & 1 else by
                to = ((i >> 1) + step) % ring * 2 + (i & 1)
                pairs.append((i * n_col + j, to * n_col + j))
        return lax.ppermute(piece, ("row", "col"), pairs)

    def over(piece, name):
        with jax.named_scope(name):
            return lax.ppermute(piece, "row", flip_x)

    sibling = lax.ppermute(own, "col", flip_core)
    both = jnp.concatenate([own, sibling])
    with jax.named_scope("z_one"):
        one = onward(both, 1)
    with jax.named_scope("z_two"):
        two = onward(both, 2)
    dense = None
    if build is not None:
        two, dense = lax.optimization_barrier((two, build(sibling)))
        over_near = [over(jnp.concatenate([own, one, two]), "x_near")]
    else:
        two, over_own = lax.optimization_barrier((two, over(own, "x_own")))
        over_near = [over_own, over(one, "x_one"), over(two, "x_two")]
    with jax.named_scope("z_three"):
        three = onward(two, 1)
    with jax.named_scope("z_four"):
        four = onward(two[:rows], 2)
    far = jnp.concatenate([three, four])
    return [own, one, two, far] + over_near, [over(far, "x_far")], dense


def per_device(embedding, tiles, tile_rows, tile_cols, counts):
    n_row = lax.axis_size("row")
    n_col = lax.axis_size("col")
    per_dev, width = embedding.shape
    flip_core = [(j, j ^ 1) for j in range(n_col)]
    groups = [list(range(core, n_col, 2)) for core in range(2)]

    meta = jnp.stack([lax.axis_index("row"), lax.axis_index("col")]).astype(jnp.int32)
    own_at = jnp.concatenate([tile_rows[0, 0], tile_cols[0, 0], counts[0]])
    sib_at = lax.ppermute(own_at, "col", flip_core)

    def build(ready):
        own_tiles, ready = lax.optimization_barrier((tiles[0, 0], ready))
        sib_tiles = lax.ppermute(own_tiles, "col", flip_core)
        return build_dense(own_at, sib_at, meta, tiles[0, 0], sib_tiles, n_row, n_col)

    early, late, dense = gather_pieces(embedding.astype(jnp.bfloat16), n_row, n_col, build)
    total = embedding
    for layer in range(LAYERS):
        head = head_multiply(dense, early)
        theirs = tail_multiply(dense, head, late, 1, jnp.bfloat16)
        arrived = lax.ppermute(theirs, "col", flip_core)
        mine = tail_multiply(dense, head, late, 0, jnp.float32)
        pair = (mine + arrived.astype(jnp.float32)).astype(jnp.bfloat16)
        parts = lax.all_to_all(
            pair.reshape(n_col // 2, per_dev, width), "col", split_axis=0, concat_axis=0, axis_index_groups=groups
        )
        current = jnp.sum(parts.astype(jnp.float32), axis=0)
        total = total + current
        if layer + 1 < LAYERS:
            early, late, _ = gather_pieces(current.astype(jnp.bfloat16), n_row, n_col)
    return total / (LAYERS + 1.0)


def solution(mesh):
    return jax.shard_map(
        per_device,
        mesh=mesh,
        in_specs=(
            P(("row", "col"), None),
            P("row", "col", None, None, None),
            P("row", "col", None),
            P("row", "col", None),
            P("row", "col"),
        ),
        out_specs=P(("row", "col"), None),
        check_vma=False,
    )
```
